128 devices in a mesh: seq: 64 (over x_lo, z, y, core), rep: 2 (over x_hi).
Axes of the slice: x: 4 (x_hi: 2, x_lo: 2; x = x_hi * 2 + x_lo), y: 4, z: 4, core: 2. Of those that a mesh axis runs over, the one named last changes fastest.
Arguments:
- clip_tokens: bfloat16 [2, 64, 256, 1152], P('rep', 'seq'), may hold values from -6 to 6
- modulation: float32 [2, 6, 1152], P('rep'), may hold values from -1 to 1
- spatial_weights: bfloat16 [4608, 1152], replicated, may hold values from -2 to 2, as said below
- temporal_weights: bfloat16 [4608, 1152], replicated, may hold values from -2 to 2, as said below
- out_cotangent: bfloat16 [2, 64, 256, 1152], P('rep', 'seq'), may hold values from -4 to 4
Outputs:
- input_grad: bfloat16 [2, 64, 256, 1152], P('rep', 'seq')
- qkv_weight_grad: float32 [3456, 1152], P(('seq', 'rep'))
- proj_weight_grad: float32 [1152, 1152], P(('seq', 'rep'))
The draws below stay inside these ranges and needn't reach their ends.
Inputs may be any that keep to these rules, and one draw needn't show every extreme that they name: `spatial_weights`: rows are the q, k, v and output projections (1152 rows each); each row multiplies a vector of 1152 features. `temporal_weights`: rows are the q, k, v and output projections (1152 rows each); each row multiplies a vector of 1152 features.
All inputs are finite; a program needn't handle non-finite values.
Results may differ from the reference program's by a relative error of at most 0.04.
Values may be sent and summed in bfloat16 or wider, within the bound.
No kernel may reach another device: no remote copies, remote signals or barrier semaphores. Data moves between devices by JAX's collectives and lax.ppermute only.
A program may use at most 128 MiB of HBM per device.

```python
import jax
import jax.numpy as jnp
from jax import lax

D = 1152
HEADS = 16
S = 256
FRAMES = 64
CLIPS = 2


def base_rows(key):
    return jnp.clip(jax.random.normal(key, (4 * D, D), jnp.float32), -4.0, 4.0) * D ** (-0.5)


def draw_spatial_weights(key, part):
    key = jax.random.fold_in(key, 5)
    values = base_rows(key)
    return jnp.clip(values, -2.0, 2.0).astype(jnp.bfloat16)


def draw_temporal_weights(key, part):
    key = jax.random.fold_in(key, 9)
    values = base_rows(key)
    return jnp.clip(values, -2.0, 2.0).astype(jnp.bfloat16)


def with_spikes(array, own_key, source, target, parts, factor):
    owner, partner = [(jnp.arange(array.shape[position]) // (array.shape[position] // parts)).reshape([-1 if axis == position else 1 for axis in range(array.ndim)]) for position in (source, target)]
    chosen = jax.random.permutation(own_key, parts)[partner]
    strong = (owner == chosen) | (owner == (partner + parts // 2) % parts)
    return jnp.where(strong, factor * array, array)


def shard_levels(key, extent, cuts, smallest, high):
    factor_of = 1.0
    for position, blocks in cuts:
        steps = jax.random.uniform(jax.random.fold_in(jax.random.fold_in(key, 6), position), (blocks,), jnp.float32, smallest / len(cuts), high / len(cuts))
        factor_of = factor_of * jnp.repeat(jnp.exp(steps), extent[position] // blocks).reshape((-1,) + (1,) * (len(extent) - 1 - position))
    return factor_of


def gaussian(stream_key, extent, width, limit, cuts=(), kind=jnp.bfloat16):
    gain = shard_levels(stream_key, extent, cuts, -0.22, 0.18) if cuts else 1.0
    array = jax.random.normal(stream_key, extent, jnp.float32) * width * gain
    return jnp.minimum(jnp.maximum(array, -limit), limit).astype(kind)


def gaussian_with(stream_key, dims, deviation, bound, cuts, heavy, kind=jnp.bfloat16):
    drawn = deviation * jax.random.normal(stream_key, dims, jnp.float32)
    if cuts:
        drawn = drawn * shard_levels(stream_key, dims, cuts, -0.22, 0.18)
    return jnp.clip(with_spikes(drawn, jax.random.fold_in(stream_key, 3), *heavy), -bound, bound).astype(kind)


def setup_inputs(seed: int = 0) -> dict:
    splits = jax.random.split(jax.random.key(seed), 6)
    return {
        "clip_tokens": gaussian(splits[0], (CLIPS, FRAMES, S, D), 1.0, 6.0, ((0, 2), (1, 64))),
        "modulation": jnp.clip(jax.random.uniform(splits[1], (CLIPS, 6, D), jnp.float32, -1.0, 1.0) * shard_levels(splits[1], (CLIPS, 6, D), ((0, 2),), -0.4, 0.0), -1.0, 1.0),
        "spatial_weights": draw_spatial_weights(jax.random.fold_in(splits[5], 71), 0),
        "temporal_weights": draw_temporal_weights(jax.random.fold_in(splits[5], 71), 0),
        "out_cotangent": gaussian_with(splits[4], (CLIPS, FRAMES, S, D), 0.25, 4.0, ((0, 2), (1, 64)), (1, 3, 64, 4.0)),
    }


def rounded(values):
    return lax.optimization_barrier(values.astype(jnp.bfloat16))

def normalize(tokens):
    values = tokens.astype(jnp.float32)
    center = values - lax.optimization_barrier(jnp.mean(values, axis=-1, keepdims=True))
    spread = lax.rsqrt(lax.optimization_barrier(jnp.mean(center * center, axis=-1, keepdims=True)) + 1e-06)
    return (center * spread, spread)

def norm_back(grad_hidden, normed, spread, gain_term):
    grad_norm = grad_hidden * (1.0 + gain_term)
    centered = grad_norm - lax.optimization_barrier(jnp.mean(grad_norm, axis=-1, keepdims=True))
    return spread * (centered - normed * lax.optimization_barrier(jnp.mean(grad_norm * normed, axis=-1, keepdims=True)))

def project(tokens, weight):
    flat_rows = tokens.reshape(-1, tokens.shape[-1])
    result = jnp.dot(flat_rows, weight.T, preferred_element_type=jnp.float32)
    return result.reshape(tokens.shape[:-1] + (weight.shape[0],))

def project_back(gradient, weight):
    flat_rows = gradient.reshape(-1, gradient.shape[-1])
    result = jnp.dot(flat_rows, weight, preferred_element_type=jnp.float32)
    return result.reshape(gradient.shape[:-1] + (weight.shape[1],))

def split_heads(qkv, head_count):
    dim_one, dim_two, dim_three, triple = qkv.shape
    features = triple // 3
    pieces = qkv.astype(jnp.float32).reshape(dim_one, dim_two, dim_three, 3, head_count, features // head_count)
    return (pieces[:, :, :, 0], pieces[:, :, :, 1], pieces[:, :, :, 2])

def attend(qkv, head_count):
    query_rows, key_rows, value_rows = split_heads(qkv, head_count)
    factor = query_rows.shape[-1] ** (-0.5)
    scores = jnp.einsum('albhe,ambhe->abhlm', query_rows, key_rows) * factor
    top_score = lax.optimization_barrier(jnp.max(scores, axis=-1, keepdims=True))
    raw_weight = jnp.exp(scores - top_score)
    prob_rows = raw_weight / lax.optimization_barrier(jnp.sum(raw_weight, axis=-1, keepdims=True))
    mixture = jnp.einsum('abhlm,ambhe->albhe', rounded(prob_rows).astype(jnp.float32), value_rows)
    shape_out = qkv.shape[:3] + (qkv.shape[3] // 3,)
    return (rounded(mixture).reshape(shape_out), prob_rows)

def attend_back(qkv, prob_rows, grad_attn, head_count):
    query_rows, key_rows, value_rows = split_heads(qkv, head_count)
    factor = query_rows.shape[-1] ** (-0.5)
    grad_heads = grad_attn.astype(jnp.float32).reshape(query_rows.shape)
    grad_prob = jnp.einsum('albhe,ambhe->abhlm', grad_heads, value_rows)
    inner = lax.optimization_barrier(jnp.sum(prob_rows * grad_prob, axis=-1, keepdims=True))
    grad_score = rounded(prob_rows * (grad_prob - inner)).astype(jnp.float32)
    grad_query = rounded(jnp.einsum('abhlm,ambhe->albhe', grad_score, key_rows) * factor)
    grad_key = rounded(jnp.einsum('abhlm,albhe->ambhe', grad_score, query_rows) * factor)
    prob_low = rounded(prob_rows).astype(jnp.float32)
    grad_value = rounded(jnp.einsum('abhlm,albhe->ambhe', prob_low, grad_heads))
    stacked = jnp.stack([grad_query, grad_key, grad_value], axis=3)
    return stacked.reshape(qkv.shape)

def reference(clip_tokens, modulation, spatial_weights, temporal_weights, out_cotangent):
    qkv_spatial = spatial_weights[:3 * D]
    out_spatial = spatial_weights[3 * D:]
    qkv_temporal = temporal_weights[:3 * D]
    out_temporal = temporal_weights[3 * D:]

    def one_clip(carry, inputs):
        qkv_total, proj_total = carry
        tokens, modes, cotangent = inputs
        shift_s, scale_s, gate_s = (modes[0], modes[1], modes[2])
        shift_t, scale_t, gate_t = (modes[3], modes[4], modes[5])
        normed_s, spread_s = normalize(tokens)
        hidden_s = rounded(normed_s * (1.0 + scale_s) + shift_s)
        qkv_s = rounded(project(hidden_s, qkv_spatial)).reshape(FRAMES, S, 1, 3 * D)
        attn_s, prob_s = attend(qkv_s, HEADS)
        attn_s = attn_s.reshape(FRAMES, S, D)
        middle = rounded(tokens.astype(jnp.float32) + gate_s * project(attn_s, out_spatial))
        normed_t, spread_t = normalize(middle)
        hidden_t = rounded(normed_t * (1.0 + scale_t) + shift_t)
        qkv_t = rounded(project(hidden_t, qkv_temporal)).reshape(1, FRAMES, S, 3 * D)
        attn_t, prob_t = attend(qkv_t, HEADS)
        grad_out_t = rounded(cotangent.astype(jnp.float32) * gate_t)
        proj_part = jnp.dot(grad_out_t.reshape(-1, D).T, attn_t.reshape(-1, D), preferred_element_type=jnp.float32)
        grad_attn_t = rounded(project_back(grad_out_t, out_temporal)).reshape(1, FRAMES, S, D)
        grad_qkv_t = attend_back(qkv_t, prob_t, grad_attn_t, HEADS)
        qkv_part = jnp.dot(grad_qkv_t.reshape(-1, 3 * D).T, hidden_t.reshape(-1, D), preferred_element_type=jnp.float32)
        grad_hidden_t = project_back(grad_qkv_t.reshape(FRAMES, S, 3 * D), qkv_temporal)
        grad_middle = rounded(cotangent.astype(jnp.float32) + norm_back(grad_hidden_t, normed_t, spread_t, scale_t))
        grad_out_s = rounded(grad_middle.astype(jnp.float32) * gate_s)
        grad_attn_s = rounded(project_back(grad_out_s, out_spatial)).reshape(FRAMES, S, 1, D)
        grad_qkv_s = attend_back(qkv_s, prob_s, grad_attn_s, HEADS).reshape(FRAMES, S, 3 * D)
        grad_hidden_s = project_back(grad_qkv_s, qkv_spatial)
        input_grad = grad_middle.astype(jnp.float32) + norm_back(grad_hidden_s, normed_s, spread_s, scale_s)
        return ((qkv_total + qkv_part, proj_total + proj_part), input_grad.astype(jnp.bfloat16))
    start = (jnp.zeros((3 * D, D), jnp.float32), jnp.zeros((D, D), jnp.float32))
    totals, input_grad = lax.scan(one_clip, start, (clip_tokens, modulation, out_cotangent))
    return (input_grad, totals[0], totals[1])
```

```python
import functools

import jax
import jax.numpy as jnp
import numpy as np
from jax import lax
from jax.experimental import pallas as pl
from jax.experimental.pallas import tpu as pltpu
from jax.sharding import PartitionSpec as P

HEADS = 16
HEAD = 72
D = HEADS * HEAD
T = 256
PLACE = 4
FACTOR = HEAD**-0.5
LOG2E = 1.4426950408889634
BOTH = ("seq", "rep")
Q_ROWS = 27
P_ROWS = 9
SUBS = 8
Q_CHUNK = SUBS * Q_ROWS
P_CHUNK = SUBS * P_ROWS
CHUNK = Q_CHUNK + P_CHUNK
PART = 384
bf16 = jnp.bfloat16
f32 = jnp.float32

NN = (((1,), (0,)), ((), ()))
NT = (((1,), (1,)), ((), ()))
TN = (((0,), (0,)), ((), ()))


def dot(a, b, dims=NN):
    return lax.dot_general(a, b, dims, preferred_element_type=f32)


GRAY = (0, 1, 3, 2)


def device_index(x, y, z, core):
    return ((((x % 2) * 4 + z) * 4 + y) * 2 + core) * 2 + x // 2


def all_coords():
    return [
        (x, y, z, core)
        for x in range(4)
        for y in range(4)
        for z in range(4)
        for core in range(2)
    ]


def flip_pairs(axis, bits):
    pairs = []
    for coord in all_coords():
        other = list(coord)
        other[axis] = GRAY.index(GRAY[coord[axis]] ^ (1 << bits[coord[3]]))
        pairs.append((device_index(*coord), device_index(*other)))
    return pairs


def core_pairs():
    return [(device_index(x, y, z, c), device_index(x, y, z, 1 - c)) for x, y, z, c in all_coords()]


def owner_of(core, chunk, sub):
    coord = []
    for axis in range(3):
        high, low = (chunk >> (2 - axis)) & 1, (sub >> (2 - axis)) & 1
        code = (low << 1) | high if core == 0 else (high << 1) | low
        coord.append(GRAY.index(code))
    return device_index(*coord, core)


def normalize(tokens):
    values = tokens.astype(f32)
    center = values - jnp.mean(values, axis=-1, keepdims=True)
    spread = lax.rsqrt(jnp.mean(center * center, axis=-1, keepdims=True) + 1e-06)
    return center * spread, spread


ROWS = 64


def modulated(src_ref, mod_ref, shift, scale, out_ref):
    for r in range(0, T, ROWS):
        normed, _ = normalize(src_ref[r : r + ROWS, :])
        out_ref[r : r + ROWS, :] = (
            normed * (1.0 + mod_ref[scale : scale + 1, :]) + mod_ref[shift : shift + 1, :]
        ).astype(bf16)


def norm_back_rows(src_ref, direct_ref, grad_ref, mod_ref, scale, out_ref):
    for r in range(0, T, ROWS):
        normed, spread = normalize(src_ref[r : r + ROWS, :])
        g = grad_ref[r : r + ROWS, :] * (1.0 + mod_ref[scale : scale + 1, :])
        centered = g - jnp.mean(g, axis=-1, keepdims=True)
        back = spread * (centered - normed * jnp.mean(g * normed, axis=-1, keepdims=True))
        out_ref[r : r + ROWS, :] = (direct_ref[r : r + ROWS, :].astype(f32) + back).astype(bf16)


W_ROWS = 576
W_CHUNKS = 4 * D // W_ROWS
QKV_CHUNKS = 3 * D // W_ROWS


def weight_copies(w_hbm, w_ref, sems, chunks):
    return [
        pltpu.make_async_copy(
            w_hbm.at[pl.ds(i * W_ROWS, W_ROWS), :], w_ref.at[pl.ds(i * W_ROWS, W_ROWS), :], sems.at[i]
        )
        for i in chunks
    ]


def qkv_heads(copies, w_ref, hid_ref, qkv_ref):
    per = W_ROWS // HEAD
    for i in range(QKV_CHUNKS):
        copies[i].wait()
        block = dot(w_ref[i * W_ROWS : (i + 1) * W_ROWS, :], hid_ref[...], NT)
        for j in range(per):
            qkv_ref[i * per + j] = block[j * HEAD : (j + 1) * HEAD, :].astype(bf16)


def softmax_keys(q, k, mask):
    scores = dot(k, q, TN)
    if mask is not None:
        scores = jnp.where(mask, scores, -1e30)
    top = jnp.max(scores, axis=0, keepdims=True)
    raw = jnp.exp2((scores - top) * (FACTOR * LOG2E))
    return raw * (1.0 / jnp.sum(raw, axis=0, keepdims=True))


def head_back(q, k, v, g, prob, prob_low):
    grad_prob = dot(v, g, TN)
    inner = jnp.sum(prob * grad_prob, axis=0, keepdims=True)
    grad_score = (prob * (grad_prob - inner)).astype(bf16)
    dq = dot(k, grad_score) * FACTOR
    dk = dot(q, grad_score, NT) * FACTOR
    dv = dot(g, prob_low, NT)
    return dq, dk, dv


def grad_heads(w_ref, go_ref, out_ref):
    for j in range(0, D, PART):
        block = dot(go_ref[...], w_ref[3 * D : 4 * D, j : j + PART])
        flipped = block.T
        if j == 0:
            whole = [flipped]
        else:
            whole.append(flipped)
    full = jnp.concatenate(whole, axis=0)
    for h in range(HEADS):
        out_ref[h] = full[h * HEAD : (h + 1) * HEAD, :].astype(bf16)


def spatial_forward_kernel(
    x_ref, mod_ref, w_hbm, middle_ref, qkv_ref, prob_ref, w_ref, hid_ref, attn_ref, sems
):
    copies = weight_copies(w_hbm, w_ref, sems, range(W_CHUNKS))
    for c in copies:
        c.start()
    modulated(x_ref, mod_ref, 0, 1, hid_ref)
    qkv_heads(copies, w_ref, hid_ref, qkv_ref)

    def pair(i, _):
        outs = []
        for s in range(2):
            h = 2 * i + s
            prob = softmax_keys(qkv_ref[h], qkv_ref[HEADS + h], None).astype(bf16)
            prob_ref[h] = prob
            outs.append(dot(qkv_ref[2 * HEADS + h], prob))
        rows = pl.ds(pl.multiple_of(i * 2 * HEAD, 16), 2 * HEAD)
        attn_ref[rows, :] = jnp.concatenate(outs, axis=0).astype(bf16)
        return _

    lax.fori_loop(0, HEADS // 2, pair, 0)
    for c in copies[QKV_CHUNKS:]:
        c.wait()
    for j in range(0, D, PART):
        block = dot(w_ref[3 * D + j : 3 * D + j + PART, :], attn_ref[...]).T
        cols = slice(j, j + PART)
        middle_ref[:, cols] = (
            x_ref[:, cols].astype(f32) + mod_ref[2:3, cols] * block
        ).astype(bf16)


def cotangent_kernel(cot_ref, mod_ref, w_hbm, heads_ref, lp_ref, w_ref, go_ref, gof_ref, tmp_ref, sems):
    copies = weight_copies(w_hbm, w_ref, sems, range(QKV_CHUNKS, W_CHUNKS))
    for c in copies:
        c.start()
    for r in range(0, T, ROWS):
        go_ref[r : r + ROWS, :] = (
            cot_ref[r : r + ROWS, :].astype(f32) * mod_ref[5:6, :]
        ).astype(bf16)
    for j in range(0, D, PART):
        gof_ref[j : j + PART, :] = go_ref[:, j : j + PART].astype(f32).T
    gather_rows(gof_ref, tmp_ref, lp_ref, P_ROWS)
    for c in copies:
        c.wait()
    grad_heads(w_ref, go_ref, heads_ref)


def gather_rows(src_ref, tmp_ref, out_ref, rows):
    for core in range(2):
        for chunk in range(SUBS):
            slot = (core * SUBS + chunk) % 2
            for sub in range(SUBS):
                start = rows * owner_of(core, chunk, sub)
                tmp_ref[slot, rows * sub : rows * (sub + 1), :] = src_ref[start : start + rows, :]
            out_ref[core * SUBS + chunk] = tmp_ref[slot].astype(bf16)


def temporal_kernel(
    m_ref, cot_ref, g_ref, mod_ref, w_hbm,
    gm_ref, hid_ref, attn_out_ref, lq_ref,
    w_ref, qkv_ref, attn_ref, grad_ref, gh_ref, tmp_ref, sems,
):
    copies = weight_copies(w_hbm, w_ref, sems, range(QKV_CHUNKS))
    for c in copies:
        c.start()
    modulated(m_ref, mod_ref, 3, 4, hid_ref)
    qkv_heads(copies, w_ref, hid_ref, qkv_ref)
    one = lax.broadcasted_iota(jnp.int32, (T, T), 0)
    two = lax.broadcasted_iota(jnp.int32, (T, T), 1)
    mask = (one & (PLACE - 1)) == (two & (PLACE - 1))

    def pair(i, _):
        outs, grads = [], []
        for s in range(2):
            h = 2 * i + s
            q, k, v, g = qkv_ref[h], qkv_ref[HEADS + h], qkv_ref[2 * HEADS + h], g_ref[h]
            prob = softmax_keys(q, k, mask)
            low = prob.astype(bf16)
            outs.append(dot(v, low))
            grads.append(head_back(q, k, v, g, prob, low))
        rows = pl.ds(pl.multiple_of(i * 2 * HEAD, 16), 2 * HEAD)
        attn_ref[rows, :] = jnp.concatenate(outs, axis=0)
        for n in range(3):
            rows = pl.ds(pl.multiple_of(n * D + i * 2 * HEAD, 16), 2 * HEAD)
            grad_ref[rows, :] = jnp.concatenate([grads[0][n], grads[1][n]], axis=0)
        return _

    lax.fori_loop(0, HEADS // 2, pair, 0)
    for n in range(3):
        rows = slice(n * D, (n + 1) * D)
        part = dot(grad_ref[rows, :].astype(bf16).T, w_ref[rows, :])
        gh_ref[...] = part if n == 0 else gh_ref[...] + part
    norm_back_rows(m_ref, cot_ref, gh_ref, mod_ref, 4, gm_ref)
    attn_out_ref[...] = attn_ref[...].astype(bf16).T
    gather_rows(grad_ref, tmp_ref, lq_ref, Q_ROWS)


def weight_grad_kernel(tbl_ref, lq_ref, lq2_ref, lp_ref, lp2_ref, hid_ref, hid2_ref, attn_ref, attn2_ref, out_ref):
    core = tbl_ref[12]
    for p in range(3):
        cols = slice(p * PART, (p + 1) * PART)

        def chunk(i, _, p=p, cols=cols):
            j = tbl_ref[p * 4 + i]
            mine = core * SUBS + j
            q = dot(lq_ref[mine], hid_ref[:, cols]) + dot(lq2_ref[j], hid2_ref[:, cols])
            o = dot(lp_ref[mine], attn_ref[:, cols]) + dot(lp2_ref[j], attn2_ref[:, cols])
            out_ref[p * 4 + i] = jnp.concatenate([q, o], axis=0).astype(bf16)
            return _

        lax.fori_loop(0, 4, chunk, 0)


def spatial_back_kernel(
    gm_ref, x_ref, mod_ref, qkv_ref, prob_ref, w_hbm, out_ref,
    w_ref, go_ref, g_ref, grad_ref, gh_ref, sems,
):
    copies = weight_copies(w_hbm, w_ref, sems, range(W_CHUNKS))
    for c in copies[QKV_CHUNKS:] + copies[:QKV_CHUNKS]:
        c.start()
    for r in range(0, T, ROWS):
        go_ref[r : r + ROWS, :] = (
            gm_ref[r : r + ROWS, :].astype(f32) * mod_ref[2:3, :]
        ).astype(bf16)
    for c in copies[QKV_CHUNKS:]:
        c.wait()
    grad_heads(w_ref, go_ref, g_ref)

    def pair(i, _):
        grads = []
        for s in range(2):
            h = 2 * i + s
            low = prob_ref[h]
            grads.append(
                head_back(
                    qkv_ref[h], qkv_ref[HEADS + h], qkv_ref[2 * HEADS + h], g_ref[h], low.astype(f32), low
                )
            )
        for n in range(3):
            rows = pl.ds(pl.multiple_of(n * D + i * 2 * HEAD, 16), 2 * HEAD)
            grad_ref[rows, :] = jnp.concatenate([grads[0][n], grads[1][n]], axis=0).astype(bf16)
        return _

    lax.fori_loop(0, HEADS // 2, pair, 0)
    for c in copies[:QKV_CHUNKS]:
        c.wait()
    for n in range(3):
        rows = slice(n * D, (n + 1) * D)
        part = dot(grad_ref[rows, :].T, w_ref[rows, :])
        gh_ref[...] = part if n == 0 else gh_ref[...] + part
    norm_back_rows(x_ref, gm_ref, gh_ref, mod_ref, 1, out_ref)


VMEM = pl.BlockSpec(memory_space=pltpu.VMEM)
ANY = pl.BlockSpec(memory_space=pl.ANY)
SMEM = pl.BlockSpec(memory_space=pltpu.SMEM)


def call(kernel, outs, scratch, specs, flops, name):
    return pl.pallas_call(
        kernel,
        out_shape=[jax.ShapeDtypeStruct(s, d) for s, d in outs],
        in_specs=specs,
        out_specs=[VMEM] * len(outs),
        scratch_shapes=scratch,
        compiler_params=pltpu.CompilerParams(vmem_limit_bytes=56 * 1024 * 1024),
        cost_estimate=pl.CostEstimate(flops=flops, bytes_accessed=12_000_000, transcendentals=0),
        name=name,
    )


WEIGHT = pltpu.VMEM((4 * D, D), bf16)
SEMS = pltpu.SemaphoreType.DMA((W_CHUNKS,))


def spatial_forward(x, mod, w):
    return call(
        spatial_forward_kernel,
        [((T, D), bf16), ((3 * HEADS, HEAD, T), bf16), ((HEADS, T, T), bf16)],
        [WEIGHT, pltpu.VMEM((T, D), bf16), pltpu.VMEM((D, T), bf16), SEMS],
        [VMEM, VMEM, ANY],
        6_000_000_000,
        "spatial_forward",
    )(x, mod, w)


def cotangent(cot, mod, w):
    return call(
        cotangent_kernel,
        [((HEADS, HEAD, T), bf16), ((2 * SUBS, P_CHUNK, T), bf16)],
        [WEIGHT, pltpu.VMEM((T, D), bf16), pltpu.VMEM((D, T), f32), pltpu.VMEM((2, P_CHUNK, T), f32), SEMS],
        [VMEM, VMEM, ANY],
        2_000_000_000,
        "cotangent_heads",
    )(cot, mod, w)


def temporal(m, cot, g, mod, w):
    return call(
        temporal_kernel,
        [((T, D), bf16), ((T, D), bf16), ((T, D), bf16), ((2 * SUBS, Q_CHUNK, T), bf16)],
        [
            WEIGHT,
            pltpu.VMEM((3 * HEADS, HEAD, T), bf16),
            pltpu.VMEM((D, T), f32),
            pltpu.VMEM((3 * D, T), f32),
            pltpu.VMEM((T, D), f32),
            pltpu.VMEM((2, Q_CHUNK, T), f32),
            SEMS,
        ],
        [VMEM, VMEM, VMEM, VMEM, ANY],
        12_000_000_000,
        "temporal_sublayer",
    )(m, cot, g, mod, w)


def weight_grad(tbl, *operands):
    return call(
        weight_grad_kernel,
        [((12, CHUNK, PART), bf16)],
        [],
        [SMEM] + [VMEM] * 8,
        2_000_000_000,
        "weight_grad",
    )(tbl, *operands)[0]


def spatial_back(gm, x, mod, qkv, prob, w):
    return call(
        spatial_back_kernel,
        [((T, D), bf16)],
        [
            WEIGHT,
            pltpu.VMEM((T, D), bf16),
            pltpu.VMEM((HEADS, HEAD, T), bf16),
            pltpu.VMEM((3 * D, T), bf16),
            pltpu.VMEM((T, D), f32),
            SEMS,
        ],
        [VMEM] * 5 + [ANY],
        8_000_000_000,
        "spatial_back",
    )(gm, x, mod, qkv, prob, w)[0]


def swap_positions(tokens):
    return lax.all_to_all(tokens.reshape(64, PLACE, D), "seq", 0, 0, tiled=True).reshape(T, D)


def pick(array, index):
    return lax.dynamic_index_in_dim(array, index, 0, keepdims=False)


def summed(a, b):
    return (a.astype(f32) + b.astype(f32)).astype(bf16)


def reduce_rows(send, keep, bits, low_bits):
    parts = []
    for p in range(3):
        got = lax.ppermute(send[4 * p : 4 * p + 4], BOTH, flip_pairs(p, (0, 1)))
        parts.append((keep[4 * p : 4 * p + 4], got))
    for step in (1, 2):
        shape = (2, 4 >> step, CHUNK, PART)
        nexts = []
        for p in range(3):
            axis = (p + step) % 3
            own, got = (v.reshape(shape) for v in parts[p])
            out = summed(pick(own, 1 - bits[axis]), pick(got, 1 - bits[axis]))
            moved = lax.ppermute(out, BOTH, flip_pairs(axis, (0, 1)))
            nexts.append((summed(pick(own, bits[axis]), pick(got, bits[axis])), moved))
        parts = nexts
    rows = jnp.concatenate([summed(a, b).reshape(CHUNK, PART) for a, b in parts], axis=1)
    rows = jnp.concatenate(
        [rows[:Q_CHUNK].reshape(SUBS, Q_ROWS, D), rows[Q_CHUNK:].reshape(SUBS, P_ROWS, D)], axis=1
    )
    for axis in range(3):
        rows = rows.reshape(2, SUBS >> (axis + 1), Q_ROWS + P_ROWS, D)
        moved = lax.ppermute(pick(rows, 1 - low_bits[axis]), BOTH, flip_pairs(axis, (1, 0)))
        rows = pick(rows, low_bits[axis]).astype(f32) + moved.astype(f32)
        if axis < 2:
            rows = rows.astype(bf16)
    rows = rows.reshape(Q_ROWS + P_ROWS, D)
    return rows[:Q_ROWS], rows[Q_ROWS:]


def on_device(clip_tokens, modulation, spatial_weights, temporal_weights, out_cotangent):
    x = clip_tokens.reshape(T, D)
    cot = out_cotangent.reshape(T, D)
    mod = modulation.reshape(6, D)
    seq = lax.axis_index("seq")
    core = seq % 2
    ring = (lax.axis_index("rep") * 2 + seq // 32, (seq // 2) % 4, (seq // 8) % 4)
    codes = [v ^ (v >> 1) for v in ring]
    first = [jnp.where(core == 0, v & 1, v >> 1) for v in codes]
    last = [jnp.where(core == 0, v >> 1, v & 1) for v in codes]

    cot_pos = swap_positions(cot)
    middle, qkv_s, prob_s = spatial_forward(x, mod, spatial_weights)
    middle_pos = swap_positions(middle)
    grad_attn, left_p = cotangent(cot_pos, mod, temporal_weights)
    gm_pos, hidden, attn, left_q = temporal(middle_pos, cot_pos, grad_attn, mod, temporal_weights)
    gm = swap_positions(gm_pos)

    def other(v):
        return lax.ppermute(v, BOTH, core_pairs())

    def theirs(v):
        return other(pick(v.reshape((2, SUBS) + v.shape[1:]), 1 - core))

    operands = (left_q, theirs(left_q), left_p, theirs(left_p), hidden, other(hidden), attn, other(attn))
    tables = []
    for send in (1, 0):
        entries = []
        for p in range(3):
            for i in range(4):
                b = [None] * 3
                b[p] = first[p] ^ send
                b[(p + 1) % 3] = i >> 1
                b[(p + 2) % 3] = i & 1
                entries.append(4 * b[0] + 2 * b[1] + b[2])
        tables.append(jnp.stack(entries + [core]).astype(jnp.int32))
    send = weight_grad(tables[0], *operands)
    keep = weight_grad(tables[1], *operands)
    qkv_rows, proj_rows = reduce_rows(send, keep, first, last)
    input_grad = spatial_back(gm, x, mod, qkv_s, prob_s, spatial_weights)
    return input_grad.reshape(clip_tokens.shape), qkv_rows, proj_rows


def solution(mesh):
    placed = (
        P("rep", "seq", None, None),
        P("rep", None, None),
        P(),
        P(),
        P("rep", "seq", None, None),
    )
    return jax.shard_map(
        on_device,
        mesh=mesh,
        in_specs=placed,
        out_specs=(P("rep", "seq", None, None), P(BOTH, None), P(BOTH, None)),
        check_vma=False,
    )
```

```python
import functools

import jax
import jax.numpy as jnp
import numpy as np
from jax import lax
from jax.experimental import pallas as pl
from jax.experimental.pallas import tpu as pltpu
from jax.sharding import PartitionSpec as P

HEADS = 16
HEAD = 72
D = HEADS * HEAD
T = 256
PLACE = 4
FACTOR = HEAD**-0.5
LOG2E = 1.4426950408889634
BOTH = ("seq", "rep")
Q_ROWS = 27
P_ROWS = 9
SUBS = 8
Q_CHUNK = SUBS * Q_ROWS
P_CHUNK = SUBS * P_ROWS
CHUNK = Q_CHUNK + P_CHUNK
Q_PAD = 224
P_PAD = 80
KEPT = ((280, 80, 256), jnp.bfloat16)
KEPT_RAW = ((88, 256, 256), jnp.bfloat16)
GROUP = 4
V_ROWS = 80
FRAMES = 64
PART = 384
bf16 = jnp.bfloat16
f32 = jnp.float32

NN = (((1,), (0,)), ((), ()))
NT = (((1,), (1,)), ((), ()))
TN = (((0,), (0,)), ((), ()))


def dot(a, b, dims=NN):
    return lax.dot_general(a, b, dims, preferred_element_type=f32)


GRAY = (0, 1, 3, 2)


def device_index(x, y, z, core):
    return ((((x % 2) * 4 + z) * 4 + y) * 2 + core) * 2 + x // 2


def all_coords():
    return [
        (x, y, z, core)
        for x in range(4)
        for y in range(4)
        for z in range(4)
        for core in range(2)
    ]


def flip_pairs(axis, bits):
    pairs = []
    for coord in all_coords():
        other = list(coord)
        other[axis] = GRAY.index(GRAY[coord[axis]] ^ (1 << bits[coord[3]]))
        pairs.append((device_index(*coord), device_index(*other)))
    return pairs


def core_pairs():
    return [(device_index(x, y, z, c), device_index(x, y, z, 1 - c)) for x, y, z, c in all_coords()]


def owner_of(core, chunk, sub):
    coord = []
    for axis in range(3):
        high, low = (chunk >> (2 - axis)) & 1, (sub >> (2 - axis)) & 1
        code = (low << 1) | high if core == 0 else (high << 1) | low
        coord.append(GRAY.index(code))
    return device_index(*coord, core)


def normalize(tokens):
    values = tokens.astype(f32)
    center = values - jnp.mean(values, axis=-1, keepdims=True)
    spread = lax.rsqrt(jnp.mean(center * center, axis=-1, keepdims=True) + 1e-06)
    return center * spread, spread


ROWS = 64


def modulated(src_ref, mod_ref, shift, scale, out_ref):
    for r in range(0, T, ROWS):
        normed, _ = normalize(src_ref[r : r + ROWS, :])
        out_ref[r : r + ROWS, :] = (
            normed * (1.0 + mod_ref[scale : scale + 1, :]) + mod_ref[shift : shift + 1, :]
        ).astype(bf16)


def norm_back_rows(src_ref, direct_ref, grad_ref, mod_ref, scale, out_ref):
    for r in range(0, T, ROWS):
        normed, spread = normalize(src_ref[r : r + ROWS, :])
        g = grad_ref[r : r + ROWS, :] * (1.0 + mod_ref[scale : scale + 1, :])
        centered = g - jnp.mean(g, axis=-1, keepdims=True)
        back = spread * (centered - normed * jnp.mean(g * normed, axis=-1, keepdims=True))
        out_ref[r : r + ROWS, :] = (direct_ref[r : r + ROWS, :].astype(f32) + back).astype(bf16)


W_ROWS = 576
W_CHUNKS = 4 * D // W_ROWS
QKV_CHUNKS = 3 * D // W_ROWS


def weight_copies(w_hbm, w_ref, sems, chunks):
    return [
        pltpu.make_async_copy(
            w_hbm.at[pl.ds(i * W_ROWS, W_ROWS), :],
            w_ref.at[pl.ds((i - chunks[0]) * W_ROWS, W_ROWS), :],
            sems.at[i],
        )
        for i in chunks
    ]


def qkv_heads(copies, w_ref, hid_ref, qk_ref, v_ref):
    per = W_ROWS // HEAD
    for i in range(QKV_CHUNKS):
        copies[i].wait()
        block = dot(w_ref[i * W_ROWS : (i + 1) * W_ROWS, :], hid_ref[...], NT)
        for j in range(per):
            h = i * per + j
            rows = block[j * HEAD : (j + 1) * HEAD, :]
            if h < HEADS:
                qk_ref[h, :HEAD] = (rows * (FACTOR * LOG2E)).astype(bf16)
            elif h < 2 * HEADS:
                qk_ref[h, :HEAD] = rows.astype(bf16)
            else:
                v_ref[h - 2 * HEADS, :HEAD] = rows.astype(bf16)


def score_grads(q, k, grad_score):
    return dot(k, grad_score) * FACTOR, dot(q, grad_score, NT) * (1.0 / LOG2E)


def grad_heads(w_ref, go_ref, out_ref):
    block = dot(go_ref[...], w_ref[...]).T
    for h in range(HEADS):
        out_ref[h] = block[h * HEAD : (h + 1) * HEAD, :].astype(bf16)


def spatial_forward_kernel(
    x_ref, mod_ref, w_hbm,
    middle_ref, kept_out, raw_out, inv_ref,
    w_ref, hid_ref, attn_ref, qk_ref, v_ref, o_ref, raw_ref, sems, out_sems,
):
    copies = weight_copies(w_hbm, w_ref, sems, range(W_CHUNKS))
    for c in copies:
        c.start()
    v_ref[:, HEAD:V_ROWS, :] = jnp.ones((HEADS, V_ROWS - HEAD, T), bf16)
    modulated(x_ref, mod_ref, 0, 1, hid_ref)
    qkv_heads(copies, w_ref, hid_ref, qk_ref, v_ref)
    kept = [
        pltpu.make_async_copy(qk_ref, kept_out.at[pl.ds(0, 2 * HEADS)], out_sems.at[0]),
        pltpu.make_async_copy(v_ref, kept_out.at[pl.ds(2 * HEADS, HEADS)], out_sems.at[1]),
    ]
    for c in kept:
        c.start()

    def raw_copy(i):
        part = pl.ds(i * GROUP, GROUP)
        return pltpu.make_async_copy(raw_ref.at[part], raw_out.at[part], out_sems.at[3 + i])

    def group(i, _):
        heads = [i * GROUP + s for s in range(GROUP)]
        scores = [dot(qk_ref[HEADS + h, :HEAD], qk_ref[h, :HEAD], TN) for h in heads]
        raws = []
        for h, sc in zip(heads, scores):
            raws.append(jnp.exp2(sc - jnp.max(sc, axis=0, keepdims=True)).astype(bf16))
            raw_ref[h] = raws[-1]
        raw_copy(i).start()
        for h, raw in zip(heads, raws):
            mixed = dot(v_ref[h], raw)
            inv = 1.0 / mixed[HEAD : HEAD + 1]
            inv_ref[h] = inv
            out = mixed[:HEAD] * inv
            o_ref[h, :HEAD] = out.astype(bf16)
            attn_ref[pl.ds(pl.multiple_of(h * HEAD, 8), HEAD), :] = out
        return _

    lax.fori_loop(0, HEADS // GROUP, group, 0)
    kept.append(pltpu.make_async_copy(o_ref, kept_out.at[pl.ds(3 * HEADS, HEADS)], out_sems.at[2]))
    kept[-1].start()
    for c in copies[QKV_CHUNKS:]:
        c.wait()
    block = dot(w_ref[3 * D :, :], attn_ref[...].astype(bf16)).T
    middle_ref[...] = (x_ref[...].astype(f32) + mod_ref[2:3, :] * block).astype(bf16)
    for c in kept + [raw_copy(i) for i in range(HEADS // GROUP)]:
        c.wait()


def cotangent_kernel(
    cot_ref, mod_ref, w_hbm, heads_ref, mine_ref, theirs_ref, w_ref, go_ref, gof_ref, tmp_ref, sems
):
    copies = weight_copies(w_hbm, w_ref, sems, range(QKV_CHUNKS, W_CHUNKS))
    for c in copies:
        c.start()
    for r in range(0, T, ROWS):
        go_ref[r : r + ROWS, :] = (
            cot_ref[r : r + ROWS, :].astype(f32) * mod_ref[5:6, :]
        ).astype(bf16)
    for j in range(0, D, PART):
        gof_ref[j : j + PART, :] = go_ref[:, j : j + PART].astype(f32).T
    gather_rows(gof_ref, tmp_ref, mine_ref, theirs_ref, P_ROWS)
    for c in copies:
        c.wait()
    grad_heads(w_ref, go_ref, heads_ref)


def gather_rows(src_ref, tmp_ref, mine_ref, theirs_ref, rows):
    me = lax.axis_index("seq") % 2
    tmp_ref[...] = jnp.zeros_like(tmp_ref)
    for core in range(2):
        for chunk in range(SUBS):
            slot = (core * SUBS + chunk) % 2
            for sub in range(SUBS):
                start = rows * owner_of(core, chunk, sub)
                tmp_ref[slot, rows * sub : rows * (sub + 1), :] = src_ref[start : start + rows, :]
            low = tmp_ref[slot].astype(bf16)

            @pl.when(me == core)
            def _(chunk=chunk, low=low):
                mine_ref[chunk] = low

            @pl.when(me != core)
            def _(chunk=chunk, low=low):
                theirs_ref[chunk] = low


def temporal_kernel(
    m_ref, cot_ref, g_ref, mod_ref, w_hbm,
    gm_ref, hid_ref, attn_out_ref, mine_ref, theirs_ref,
    w_ref, qk_ref, v_ref, attn_ref, grad_ref, gh_ref, tmp_ref, sems,
):
    copies = weight_copies(w_hbm, w_ref, sems, range(QKV_CHUNKS))
    for c in copies:
        c.start()
    modulated(m_ref, mod_ref, 3, 4, hid_ref)
    qkv_heads(copies, w_ref, hid_ref, qk_ref, v_ref)

    def group(i, _):
        heads = [i * GROUP + s for s in range(GROUP)]
        scores = [blocks(dot(qk_ref[HEADS + h, :HEAD], qk_ref[h, :HEAD], TN)) for h in heads]
        raws = [jnp.exp2(sc - jnp.max(sc, axis=0, keepdims=True)) for sc in scores]
        probs = [raw * (1.0 / jnp.sum(raw, axis=0, keepdims=True)) for raw in raws]
        lows = [spread(prob) for prob in probs]
        grad_probs = [blocks(dot(v_ref[h], g_ref[h], TN)) for h in heads]
        for h, prob, low, gp in zip(heads, probs, lows, grad_probs):
            inner = jnp.sum(prob * gp, axis=0, keepdims=True)
            grad_score = spread(prob * (gp - inner))
            dq, dk = score_grads(qk_ref[h, :HEAD], qk_ref[HEADS + h, :HEAD], grad_score)
            dv = dot(g_ref[h], low, NT)
            attn_ref[pl.ds(pl.multiple_of(h * HEAD, 8), HEAD), :] = dot(v_ref[h], low)
            for n, value in enumerate((dq, dk, dv)):
                grad_ref[pl.ds(pl.multiple_of(n * D + h * HEAD, 8), HEAD), :] = value
        return _

    lax.fori_loop(0, HEADS // GROUP, group, 0)
    gh_ref[...] = dot(grad_ref[...].astype(bf16).T, w_ref[: 3 * D, :])
    norm_back_rows(m_ref, cot_ref, gh_ref, mod_ref, 4, gm_ref)
    attn_out_ref[...] = attn_ref[...].astype(bf16).T
    gather_rows(grad_ref, tmp_ref, mine_ref, theirs_ref, Q_ROWS)


def first_lanes():
    return lax.broadcasted_iota(jnp.int32, (FRAMES, 2 * FRAMES), 1) < FRAMES


def blocks(full):
    f, lane = FRAMES, first_lanes()
    left = jnp.where(lane, full[:f, : 2 * f], full[f : 2 * f, : 2 * f])
    right = jnp.where(lane, full[2 * f : 3 * f, 2 * f :], full[3 * f :, 2 * f :])
    return jnp.concatenate([left, right], axis=1)


def spread(side):
    lane = first_lanes()
    zero = jnp.zeros((FRAMES, 2 * FRAMES), f32)
    a, b = side[:, : 2 * FRAMES], side[:, 2 * FRAMES :]
    left = jnp.concatenate([jnp.where(lane, a, zero), jnp.where(lane, zero, a), zero, zero], axis=0)
    right = jnp.concatenate([zero, zero, jnp.where(lane, b, zero), jnp.where(lane, zero, b)], axis=0)
    return jnp.concatenate([left, right], axis=1).astype(bf16)


def own_bits():
    seq, rep = lax.axis_index("seq"), lax.axis_index("rep")
    core = seq % 2
    ring = (rep * 2 + seq // 32, (seq // 2) % 4, (seq // 8) % 4)
    codes = [v ^ (v >> 1) for v in ring]
    first = [jnp.where(core == 0, v & 1, v >> 1) for v in codes]
    last = [jnp.where(core == 0, v >> 1, v & 1) for v in codes]
    return first, last


def weight_grad_kernel(
    flip,
    q1_ref, q2_ref, p1_ref, p2_ref, h1_ref, h2_ref, a1_ref, a2_ref,
    out0_ref, out1_ref, out2_ref,
    ql_ref, pl_ref, h_ref, a_ref,
):
    first, _ = own_bits()
    h_ref[:T, :] = h1_ref[...]
    h_ref[T:, :] = h2_ref[...]
    a_ref[:T, :] = a1_ref[...]
    a_ref[T:, :] = a2_ref[...]
    for p, out_ref in enumerate((out0_ref, out1_ref, out2_ref)):
        for i in range(4):
            bits = [None] * 3
            bits[p] = first[p] ^ flip
            bits[(p + 1) % 3] = i >> 1
            bits[(p + 2) % 3] = i & 1
            j = 4 * bits[0] + 2 * bits[1] + bits[2]
            rows = slice(i * Q_PAD, (i + 1) * Q_PAD)
            ql_ref[rows, :T] = q1_ref[j]
            ql_ref[rows, T:] = q2_ref[j]
            rows = slice(i * P_PAD, (i + 1) * P_PAD)
            pl_ref[rows, :T] = p1_ref[j]
            pl_ref[rows, T:] = p2_ref[j]
        cols = slice(p * PART, (p + 1) * PART)
        q = dot(ql_ref[...], h_ref[:, cols])
        o = dot(pl_ref[...], a_ref[:, cols])
        for i in range(4):
            out_ref[i] = jnp.concatenate(
                [q[i * Q_PAD : i * Q_PAD + Q_CHUNK], o[i * P_PAD : i * P_PAD + P_CHUNK]], axis=0
            ).astype(bf16)


def spatial_attention_back_kernel(
    gm_ref, mod_ref, inv_ref, kept_hbm, raw_hbm, w_hbm, grad_ref,
    w_ref, go_ref, g_ref, kept_ref, raw_ref, sems, in_sems,
):
    copies = weight_copies(w_hbm, w_ref, sems, range(QKV_CHUNKS, W_CHUNKS))
    kept = [
        pltpu.make_async_copy(kept_hbm.at[pl.ds(0, 4 * HEADS)], kept_ref, in_sems.at[0]),
        pltpu.make_async_copy(raw_hbm.at[pl.ds(0, HEADS)], raw_ref, in_sems.at[1]),
    ]
    for c in copies + kept:
        c.start()
    for r in range(0, T, ROWS):
        go_ref[r : r + ROWS, :] = (
            gm_ref[r : r + ROWS, :].astype(f32) * mod_ref[2:3, :]
        ).astype(bf16)
    for c in copies:
        c.wait()
    grad_heads(w_ref, go_ref, g_ref)
    for c in kept:
        c.wait()

    def group(i, _):
        heads = [i * GROUP + s for s in range(GROUP)]
        scaled, grad_probs, inners = [], [], []
        for h in heads:
            g = (g_ref[h].astype(f32) * inv_ref[h]).astype(bf16)
            scaled.append(g)
            out = kept_ref[3 * HEADS + h, :HEAD].astype(f32)
            inners.append(jnp.sum(g.astype(f32) * out, axis=0, keepdims=True))
            grad_probs.append(dot(kept_ref[2 * HEADS + h, :HEAD], g, TN))
        for h, g, inner, gp in zip(heads, scaled, inners, grad_probs):
            raw = raw_ref[h]
            grad_score = (raw.astype(f32) * (gp - inner)).astype(bf16)
            dq, dk = score_grads(kept_ref[h, :HEAD], kept_ref[HEADS + h, :HEAD], grad_score)
            for n, value in enumerate((dq, dk, dot(g, raw, NT))):
                grad_ref[n * HEADS + h] = value.astype(bf16)
        return _

    lax.fori_loop(0, HEADS // GROUP, group, 0)


def spatial_norm_back_kernel(grad_ref, gm_ref, x_ref, mod_ref, w_hbm, out_ref, w_ref, cat_ref, gh_ref, sems):
    copies = weight_copies(w_hbm, w_ref, sems, range(QKV_CHUNKS))
    for c in copies:
        c.start()
    for h in range(0, 3 * HEADS, 2):
        pair = jnp.concatenate([grad_ref[h].astype(f32), grad_ref[h + 1].astype(f32)], axis=0)
        cat_ref[h * HEAD : (h + 2) * HEAD, :] = pair.astype(bf16)
    flipped = cat_ref[...].T
    for c in copies:
        c.wait()
    gh_ref[...] = dot(flipped, w_ref[: 3 * D, :])
    norm_back_rows(x_ref, gm_ref, gh_ref, mod_ref, 1, out_ref)


def chunk_bits():
    first, _ = own_bits()
    return [(first[(p + 1) % 3], first[(p + 2) % 3]) for p in range(3)]


def second_send_kernel(*refs):
    keep, got, out = refs[0:3], refs[3:6], refs[7:10]
    for p, (a, _) in enumerate(chunk_bits()):
        for j in range(2):
            i = 2 * (1 - a) + j
            out[p][j] = (keep[p][i].astype(f32) + got[p][i].astype(f32)).astype(bf16)


def third_send_kernel(*refs):
    keep, got, more, out = refs[0:3], refs[3:6], refs[6:9], refs[10:13]
    for p, (a, b) in enumerate(chunk_bits()):
        i = 2 * a + 1 - b
        out[p][...] = (
            keep[p][i].astype(f32) + got[p][i].astype(f32) + more[p][1 - b].astype(f32)
        ).astype(bf16)


Q_HALVES = (Q_CHUNK // 2, Q_CHUNK // 4, Q_CHUNK // 8)
P_HALVES = (P_CHUNK // 2, P_CHUNK // 4, P_CHUNK // 8)


def split_halves(total_ref, bit, q_rows, p_rows, half_ref, keep_ref, send_ref):
    total = 2 * q_rows + 2 * p_rows
    for side in range(2):
        q, p = side * q_rows, 2 * q_rows + side * p_rows
        half_ref[side, :q_rows] = total_ref[q : q + q_rows, :]
        half_ref[side, q_rows : total // 2] = total_ref[p : p + p_rows, :]
    keep_ref[...] = half_ref[bit]
    send_ref[...] = half_ref[1 - bit].astype(bf16)


def fourth_send_kernel(*refs):
    keep, got, more, most = refs[0:3], refs[3:6], refs[6:9], refs[9:12]
    own_ref, send_ref, row_ref, half_ref = refs[12:16]
    for p, (a, b) in enumerate(chunk_bits()):
        i = 2 * a + b
        row_ref[:, p * PART : (p + 1) * PART] = (
            keep[p][i].astype(f32) + got[p][i].astype(f32) + more[p][b].astype(f32)
        ) + most[p][...].astype(f32)
    split_halves(row_ref, own_bits()[1][0], Q_HALVES[0], P_HALVES[0], half_ref, own_ref, send_ref)


def later_send_kernel(step, own_in, got_ref, own_ref, send_ref, row_ref, half_ref):
    row_ref[...] = own_in[...] + got_ref[...].astype(f32)
    split_halves(row_ref, own_bits()[1][step], Q_HALVES[step], P_HALVES[step], half_ref, own_ref, send_ref)


def last_sum_kernel(own_ref, got_ref, q_ref, p_ref):
    total = own_ref[...] + got_ref[...].astype(f32)
    q_ref[...] = total[:Q_ROWS]
    p_ref[...] = total[Q_ROWS:]


VMEM = pl.BlockSpec(memory_space=pltpu.VMEM)
ANY = pl.BlockSpec(memory_space=pl.ANY)


def call(kernel, outs, scratch, specs, flops, name, out_specs=None, limit=54):
    return pl.pallas_call(
        kernel,
        out_shape=[jax.ShapeDtypeStruct(s, d) for s, d in outs],
        in_specs=specs,
        out_specs=out_specs or [VMEM] * len(outs),
        scratch_shapes=scratch,
        compiler_params=pltpu.CompilerParams(vmem_limit_bytes=limit * 1024 * 1024),
        cost_estimate=pl.CostEstimate(flops=flops, bytes_accessed=12_000_000 if flops > 1_000_000_000 else 1_000, transcendentals=0),
        name=name,
    )


WEIGHT = pltpu.VMEM((4 * D, D), bf16)
W_QKV = pltpu.VMEM((3 * D, D), bf16)
W_OUT = pltpu.VMEM((D, D), bf16)
SEMS = pltpu.SemaphoreType.DMA((W_CHUNKS,))
QK = ((2 * HEADS, V_ROWS, T), bf16)
V = ((HEADS, V_ROWS, T), bf16)
HEAD_ROWS = ((HEADS, HEAD, T), bf16)
TOKENS = ((T, D), bf16)


RAW = ((HEADS, T, T), bf16)


def spatial_forward(x, mod, w):
    return call(
        spatial_forward_kernel,
        [TOKENS, KEPT, KEPT_RAW, ((HEADS, 1, T), f32)],
        [
            WEIGHT,
            pltpu.VMEM(*TOKENS),
            pltpu.VMEM((D, T), f32),
            pltpu.VMEM(*QK),
            pltpu.VMEM(*V),
            pltpu.VMEM(*V),
            pltpu.VMEM(*RAW),
            SEMS,
            pltpu.SemaphoreType.DMA((3 + HEADS // GROUP,)),
        ],
        [VMEM, VMEM, ANY],
        6_000_000_000,
        "spatial_forward",
        [VMEM, ANY, ANY, VMEM],
    )(x, mod, w)


def cotangent(cot, mod, w):
    rows = ((SUBS, P_PAD, T), bf16)
    return call(
        cotangent_kernel,
        [HEAD_ROWS, rows, rows],
        [W_OUT, pltpu.VMEM(*TOKENS), pltpu.VMEM((D, T), f32), pltpu.VMEM((2, P_PAD, T), f32), SEMS],
        [VMEM, VMEM, ANY],
        2_000_000_000,
        "cotangent_heads",
    )(cot, mod, w)


def temporal(m, cot, g, mod, w):
    rows = ((SUBS, Q_PAD, T), bf16)
    return call(
        temporal_kernel,
        [TOKENS, TOKENS, TOKENS, rows, rows],
        [
            W_QKV,
            pltpu.VMEM(*QK),
            pltpu.VMEM(*HEAD_ROWS),
            pltpu.VMEM((D, T), f32),
            pltpu.VMEM((3 * D, T), f32),
            pltpu.VMEM((T, D), f32),
            pltpu.VMEM((2, Q_PAD, T), f32),
            SEMS,
        ],
        [VMEM, VMEM, VMEM, VMEM, ANY],
        12_000_000_000,
        "temporal_sublayer",
    )(m, cot, g, mod, w)


def weight_grad(flip, *operands):
    return call(
        functools.partial(weight_grad_kernel, flip),
        [((4, CHUNK, PART), bf16)] * 3,
        [
            pltpu.VMEM((4 * Q_PAD, 2 * T), bf16),
            pltpu.VMEM((4 * P_PAD, 2 * T), bf16),
            pltpu.VMEM((2 * T, D), bf16),
            pltpu.VMEM((2 * T, D), bf16),
        ],
        [VMEM] * 8,
        10_000_000,
        "weight_grad_send" if flip else "weight_grad_keep",
        limit=20,
    )(*operands)


def spatial_attention_back(gm, mod, kept, raw, inv, w):
    return call(
        spatial_attention_back_kernel,
        [((3 * HEADS, HEAD, T), bf16)],
        [
            W_OUT,
            pltpu.VMEM(*TOKENS),
            pltpu.VMEM(*HEAD_ROWS),
            pltpu.VMEM((4 * HEADS, V_ROWS, T), bf16),
            pltpu.VMEM(*RAW),
            SEMS,
            pltpu.SemaphoreType.DMA((2,)),
        ],
        [VMEM] * 3 + [ANY] * 3,
        5_000_000_000,
        "spatial_attention_back",
    )(gm, mod, inv, kept, raw, w)[0]


def spatial_norm_back(grad, gm, x, mod, w):
    return call(
        spatial_norm_back_kernel,
        [TOKENS],
        [W_QKV, pltpu.VMEM((3 * D, T), bf16), pltpu.VMEM((T, D), f32), SEMS],
        [VMEM] * 4 + [ANY],
        5_000_000_000,
        "spatial_norm_back",
    )(grad, gm, x, mod, w)[0]


def to_positions(tokens):
    got = lax.all_to_all(tokens.reshape(FRAMES, PLACE, D), "seq", 0, 0, tiled=True)
    return got.transpose(1, 0, 2).reshape(T, D)


def to_frames(tokens):
    sent = tokens.reshape(PLACE, FRAMES, D).transpose(1, 0, 2)
    return lax.all_to_all(sent, "seq", 0, 0, tiled=True).reshape(T, D)


def reduce_rows(send, keep, before_second, before_third):
    half, one = ((2, CHUNK, PART), bf16), ((CHUNK, PART), bf16)
    got = [lax.ppermute(send[p], BOTH, flip_pairs(p, (0, 1))) for p in range(3)]
    out = call(second_send_kernel, [half] * 3, [], [VMEM] * 6 + [ANY], 1_000_000, "second_send", limit=12)(
        *keep, *got, before_second
    )
    more = [lax.ppermute(out[p], BOTH, flip_pairs((p + 1) % 3, (0, 1))) for p in range(3)]
    out = call(third_send_kernel, [one] * 3, [], [VMEM] * 9 + [ANY], 1_000_000, "third_send", limit=12)(
        *keep, *got, *more, before_third
    )
    most = [lax.ppermute(out[p], BOTH, flip_pairs((p + 2) % 3, (0, 1))) for p in range(3)]
    for step in range(3):
        rows = Q_HALVES[step] + P_HALVES[step]
        kernel = fourth_send_kernel if step == 0 else functools.partial(later_send_kernel, step)
        operands = (*keep, *got, *more, *most) if step == 0 else (own, moved)
        own, sent = call(
            kernel,
            [((rows, D), f32), ((rows, D), bf16)],
            [pltpu.VMEM((2 * rows, D), f32), pltpu.VMEM((2, rows, D), f32)],
            [VMEM] * len(operands),
            1_000_000,
            "later_send",
            limit=16,
        )(*operands)
        moved = lax.ppermute(sent, BOTH, flip_pairs(step, (1, 0)))
    return call(
        last_sum_kernel,
        [((Q_ROWS, D), f32), ((P_ROWS, D), f32)],
        [],
        [VMEM] * 2,
        1_000_000,
        "last_sum",
        limit=8,
    )(own, moved)


def on_device(clip_tokens, modulation, spatial_weights, temporal_weights, out_cotangent):
    x = clip_tokens.reshape(T, D)
    cot = out_cotangent.reshape(T, D)
    mod = modulation.reshape(6, D)
    cot_pos = to_positions(cot)
    middle, kept, raw, inv = spatial_forward(x, mod, spatial_weights)
    middle_pos = to_positions(middle)
    grad_attn, mine_p, theirs_p = cotangent(cot_pos, mod, temporal_weights)
    gm_pos, hidden, attn, mine_q, theirs_q = temporal(
        middle_pos, cot_pos, grad_attn, mod, temporal_weights
    )
    gm = to_frames(gm_pos)

    def other(v):
        return lax.ppermute(v, BOTH, core_pairs())

    operands = (mine_q, other(theirs_q), mine_p, other(theirs_p), hidden, other(hidden), attn, other(attn))
    send = weight_grad(1, *operands)
    keep = weight_grad(0, *operands)
    grad = spatial_attention_back(gm, mod, kept, raw, inv, spatial_weights)
    input_grad = spatial_norm_back(grad, gm, x, mod, spatial_weights)
    qkv_rows, proj_rows = reduce_rows(send, keep, grad, input_grad)
    return input_grad.reshape(clip_tokens.shape), qkv_rows, proj_rows


def solution(mesh):
    placed = (
        P("rep", "seq", None, None),
        P("rep", None, None),
        P(),
        P(),
        P("rep", "seq", None, None),
    )
    return jax.shard_map(
        on_device,
        mesh=mesh,
        in_specs=placed,
        out_specs=(P("rep", "seq", None, None), P(BOTH, None), P(BOTH, None)),
        check_vma=False,
    )
```

```python
import functools

import jax
import jax.numpy as jnp
import numpy as np
from jax import lax
from jax.experimental import pallas as pl
from jax.experimental.pallas import tpu as pltpu
from jax.sharding import PartitionSpec as P

HEADS = 16
HEAD = 72
D = HEADS * HEAD
T = 256
PLACE = 4
FACTOR = HEAD**-0.5
LOG2E = 1.4426950408889634
BOTH = ("seq", "rep")
Q_ROWS = 27
P_ROWS = 9
SUBS = 8
Q_CHUNK = SUBS * Q_ROWS
P_CHUNK = SUBS * P_ROWS
CHUNK = Q_CHUNK + P_CHUNK
Q_PAD = 224
P_PAD = 80
KEPT = ((280, 80, 256), jnp.bfloat16)
KEPT_RAW = ((88, 256, 256), jnp.bfloat16)
GROUP = 4
V_ROWS = 80
FRAMES = 64
PART = 384
bf16 = jnp.bfloat16
f32 = jnp.float32

NN = (((1,), (0,)), ((), ()))
NT = (((1,), (1,)), ((), ()))
TN = (((0,), (0,)), ((), ()))


def dot(a, b, dims=NN):
    return lax.dot_general(a, b, dims, preferred_element_type=f32)


GRAY = (0, 1, 3, 2)


def device_index(x, y, z, core):
    return ((((x % 2) * 4 + z) * 4 + y) * 2 + core) * 2 + x // 2


def all_coords():
    return [
        (x, y, z, core)
        for x in range(4)
        for y in range(4)
        for z in range(4)
        for core in range(2)
    ]


def flip_pairs(axis, bits):
    pairs = []
    for coord in all_coords():
        other = list(coord)
        other[axis] = GRAY.index(GRAY[coord[axis]] ^ (1 << bits[coord[3]]))
        pairs.append((device_index(*coord), device_index(*other)))
    return pairs


def core_pairs():
    return [(device_index(x, y, z, c), device_index(x, y, z, 1 - c)) for x, y, z, c in all_coords()]


def owner_of(core, chunk, sub):
    coord = []
    for axis in range(3):
        high, low = (chunk >> (2 - axis)) & 1, (sub >> (2 - axis)) & 1
        code = (low << 1) | high if core == 0 else (high << 1) | low
        coord.append(GRAY.index(code))
    return device_index(*coord, core)


def normalize(tokens):
    values = tokens.astype(f32)
    center = values - jnp.mean(values, axis=-1, keepdims=True)
    spread = lax.rsqrt(jnp.mean(center * center, axis=-1, keepdims=True) + 1e-06)
    return center * spread, spread


ROWS = 64


def modulated(src_ref, mod_ref, shift, scale, out_ref):
    for r in range(0, T, ROWS):
        normed, _ = normalize(src_ref[r : r + ROWS, :])
        out_ref[r : r + ROWS, :] = (
            normed * (1.0 + mod_ref[scale : scale + 1, :]) + mod_ref[shift : shift + 1, :]
        ).astype(bf16)


def norm_back_rows(src_ref, direct_ref, grad_ref, mod_ref, scale, out_ref):
    for r in range(0, T, ROWS):
        normed, spread = normalize(src_ref[r : r + ROWS, :])
        g = grad_ref[r : r + ROWS, :] * (1.0 + mod_ref[scale : scale + 1, :])
        centered = g - jnp.mean(g, axis=-1, keepdims=True)
        back = spread * (centered - normed * jnp.mean(g * normed, axis=-1, keepdims=True))
        out_ref[r : r + ROWS, :] = (direct_ref[r : r + ROWS, :].astype(f32) + back).astype(bf16)


W_ROWS = 576
W_CHUNKS = 4 * D // W_ROWS
QKV_CHUNKS = 3 * D // W_ROWS


def weight_copies(w_hbm, w_ref, sems, chunks):
    return [
        pltpu.make_async_copy(
            w_hbm.at[pl.ds(i * W_ROWS, W_ROWS), :],
            w_ref.at[pl.ds((i - chunks[0]) * W_ROWS, W_ROWS), :],
            sems.at[i],
        )
        for i in chunks
    ]


AHEAD = 3


def start_weights(copies):
    for c in copies[:AHEAD]:
        c.start()


def next_weights(copies, i):
    copies[i].wait()
    if i + AHEAD < len(copies):
        copies[i + AHEAD].start()


def qkv_heads(copies, w_ref, hid_ref, qk_ref, v_ref):
    per = W_ROWS // HEAD
    for i in range(QKV_CHUNKS):
        next_weights(copies, i)
        block = dot(w_ref[i * W_ROWS : (i + 1) * W_ROWS, :], hid_ref[...], NT)
        for j in range(per):
            h = i * per + j
            rows = block[j * HEAD : (j + 1) * HEAD, :]
            if h < HEADS:
                qk_ref[h, :HEAD] = (rows * (FACTOR * LOG2E)).astype(bf16)
            elif h < 2 * HEADS:
                qk_ref[h, :HEAD] = rows.astype(bf16)
            else:
                v_ref[h - 2 * HEADS, :HEAD] = rows.astype(bf16)


def score_grads(q, k, grad_score):
    return dot(k, grad_score) * FACTOR, dot(q, grad_score, NT) * (1.0 / LOG2E)


def grad_heads(w, go, out_ref):
    block = dot(go, w).T
    for h in range(HEADS):
        out_ref[h] = block[h * HEAD : (h + 1) * HEAD, :].astype(bf16)


def spatial_forward_kernel(
    x_ref, cot_ref, mod_ref, w_hbm,
    both_ref, kept_out, raw_out, inv_ref,
    w_ref, hid_ref, attn_ref, qk_ref, v_ref, o_ref, raw_ref, sems, out_sems,
):
    copies = weight_copies(w_hbm, w_ref, sems, range(W_CHUNKS))
    start_weights(copies)
    both_ref[:, PLACE:, :] = cot_ref[...].astype(f32).reshape(FRAMES, PLACE, D).astype(bf16)
    v_ref[:, HEAD:V_ROWS, :] = jnp.ones((HEADS, V_ROWS - HEAD, T), bf16)
    modulated(x_ref, mod_ref, 0, 1, hid_ref)
    qkv_heads(copies, w_ref, hid_ref, qk_ref, v_ref)
    kept = [
        pltpu.make_async_copy(qk_ref, kept_out.at[pl.ds(0, 2 * HEADS)], out_sems.at[0]),
        pltpu.make_async_copy(v_ref, kept_out.at[pl.ds(2 * HEADS, HEADS)], out_sems.at[1]),
    ]
    for c in kept:
        c.start()

    def raw_copy(i):
        part = pl.ds(i * GROUP, GROUP)
        return pltpu.make_async_copy(raw_ref.at[part], raw_out.at[part], out_sems.at[3 + i])

    def group(i, _):
        heads = [i * GROUP + s for s in range(GROUP)]
        scores = [dot(qk_ref[HEADS + h, :HEAD], qk_ref[h, :HEAD], TN) for h in heads]
        raws = []
        for h, sc in zip(heads, scores):
            raws.append(jnp.exp2(sc - jnp.max(sc, axis=0, keepdims=True)).astype(bf16))
            raw_ref[h] = raws[-1]
        raw_copy(i).start()
        for h, raw in zip(heads, raws):
            mixed = dot(v_ref[h], raw)
            inv = 1.0 / mixed[HEAD : HEAD + 1]
            inv_ref[h] = inv
            out = mixed[:HEAD] * inv
            o_ref[h, :HEAD] = out.astype(bf16)
            attn_ref[pl.ds(pl.multiple_of(h * HEAD, 8), HEAD), :] = out
        return _

    lax.fori_loop(0, HEADS // GROUP, group, 0)
    kept.append(pltpu.make_async_copy(o_ref, kept_out.at[pl.ds(3 * HEADS, HEADS)], out_sems.at[2]))
    kept[-1].start()
    for i in range(QKV_CHUNKS, W_CHUNKS):
        next_weights(copies, i)
    block = dot(w_ref[3 * D :, :], attn_ref[...].astype(bf16)).T
    middle = x_ref[...].astype(f32) + mod_ref[2:3, :] * block
    both_ref[:, :PLACE, :] = middle.reshape(FRAMES, PLACE, D).astype(bf16)
    for c in kept + [raw_copy(i) for i in range(HEADS // GROUP)]:
        c.wait()


def gather_rows(src_ref, tmp_ref, mine_ref, theirs_ref, rows, start):
    me = lax.axis_index("seq") % 2
    padded = tmp_ref.shape[1]
    tmp_ref[...] = jnp.zeros_like(tmp_ref)
    for core in range(2):
        for chunk in range(SUBS):
            slot = (core * SUBS + chunk) % 2
            for sub in range(SUBS):
                first = rows * owner_of(core, chunk, sub)
                tmp_ref[slot, rows * sub : rows * (sub + 1), :] = src_ref[first : first + rows, :]
            low = tmp_ref[slot].astype(bf16)

            @pl.when(me == core)
            def _(chunk=chunk, low=low):
                mine_ref[chunk, start : start + padded] = low

            @pl.when(me != core)
            def _(chunk=chunk, low=low):
                theirs_ref[chunk, start : start + padded] = low


def by_position(both, start):
    row = lax.broadcasted_iota(jnp.int32, (T, 2 * T), 0)
    col = lax.broadcasted_iota(jnp.int32, (T, 2 * T), 1)
    source = (row % FRAMES) * (2 * PLACE) + row // FRAMES + start
    return dot(jnp.where(source == col, 1.0, 0.0).astype(bf16), both).astype(bf16)


def by_frame(tokens):
    row = lax.broadcasted_iota(jnp.int32, (T, T), 0)
    col = lax.broadcasted_iota(jnp.int32, (T, T), 1)
    source = (row % PLACE) * FRAMES + row // PLACE
    return dot(jnp.where(source == col, 1.0, 0.0).astype(bf16), tokens)


def temporal_kernel(
    both_ref, mod_ref, w_hbm,
    gm_out, right_ref, mine_ref, theirs_ref,
    w_ref, m_ref, cot_ref, gm_ref, hid_ref, qk_ref, v_ref, g_ref, attn_ref, grad_ref, gh_ref,
    tmp_ref, tmp_p_ref, sems,
):
    copies = weight_copies(w_hbm, w_ref, sems, range(W_CHUNKS))
    start_weights(copies)
    both = both_ref[...].reshape(2 * T, D)
    m_ref[...] = by_position(both, 0)
    modulated(m_ref, mod_ref, 3, 4, hid_ref)
    right_ref[:T, :] = hid_ref[...]
    qkv_heads(copies, w_ref, hid_ref, qk_ref, v_ref)
    cot_ref[...] = by_position(both, PLACE)
    go = (cot_ref[...].astype(f32) * mod_ref[5:6, :]).astype(bf16)
    grad_ref[:D, :] = go.astype(f32).T
    gather_rows(grad_ref, tmp_p_ref, mine_ref, theirs_ref, P_ROWS, Q_PAD)
    for i in range(QKV_CHUNKS, W_CHUNKS):
        next_weights(copies, i)
    grad_heads(w_ref[3 * D :, :], go, g_ref)

    def group(i, _):
        heads = [i * GROUP + s for s in range(GROUP)]
        scores = [blocks(dot(qk_ref[HEADS + h, :HEAD], qk_ref[h, :HEAD], TN)) for h in heads]
        raws = [jnp.exp2(sc - jnp.max(sc, axis=0, keepdims=True)) for sc in scores]
        probs = [raw * (1.0 / jnp.sum(raw, axis=0, keepdims=True)) for raw in raws]
        lows = [spread(prob) for prob in probs]
        grad_probs = [blocks(dot(v_ref[h], g_ref[h], TN)) for h in heads]
        for h, prob, low, gp in zip(heads, probs, lows, grad_probs):
            inner = jnp.sum(prob * gp, axis=0, keepdims=True)
            grad_score = spread(prob * (gp - inner))
            dq, dk = score_grads(qk_ref[h, :HEAD], qk_ref[HEADS + h, :HEAD], grad_score)
            dv = dot(g_ref[h], low, NT)
            attn_ref[pl.ds(pl.multiple_of(h * HEAD, 8), HEAD), :] = dot(v_ref[h], low)
            for n, value in enumerate((dq, dk, dv)):
                grad_ref[pl.ds(pl.multiple_of(n * D + h * HEAD, 8), HEAD), :] = value
        return _

    lax.fori_loop(0, HEADS // GROUP, group, 0)
    gh_ref[...] = dot(grad_ref[...].astype(bf16).T, w_ref[: 3 * D, :])
    norm_back_rows(m_ref, cot_ref, gh_ref, mod_ref, 4, gm_ref)
    gm_out[...] = by_frame(gm_ref[...]).reshape(FRAMES, PLACE, D).astype(bf16)
    right_ref[T:, :] = attn_ref[...].astype(bf16).T
    gather_rows(grad_ref, tmp_ref, mine_ref, theirs_ref, Q_ROWS, 0)


def first_lanes():
    return lax.broadcasted_iota(jnp.int32, (FRAMES, 2 * FRAMES), 1) < FRAMES


def blocks(full):
    f, lane = FRAMES, first_lanes()
    left = jnp.where(lane, full[:f, : 2 * f], full[f : 2 * f, : 2 * f])
    right = jnp.where(lane, full[2 * f : 3 * f, 2 * f :], full[3 * f :, 2 * f :])
    return jnp.concatenate([left, right], axis=1)


def spread(side):
    lane = first_lanes()
    zero = jnp.zeros((FRAMES, 2 * FRAMES), f32)
    a, b = side[:, : 2 * FRAMES], side[:, 2 * FRAMES :]
    left = jnp.concatenate([jnp.where(lane, a, zero), jnp.where(lane, zero, a), zero, zero], axis=0)
    right = jnp.concatenate([zero, zero, jnp.where(lane, b, zero), jnp.where(lane, zero, b)], axis=0)
    return jnp.concatenate([left, right], axis=1).astype(bf16)


def own_bits():
    seq, rep = lax.axis_index("seq"), lax.axis_index("rep")
    core = seq % 2
    ring = (rep * 2 + seq // 32, (seq // 2) % 4, (seq // 8) % 4)
    codes = [v ^ (v >> 1) for v in ring]
    first = [jnp.where(core == 0, v & 1, v >> 1) for v in codes]
    last = [jnp.where(core == 0, v >> 1, v & 1) for v in codes]
    return first, last


def weight_grad_kernel(
    flip, left1_ref, left2_ref, right1_ref, right2_ref, out0_ref, out1_ref, out2_ref, ql_ref, pl_ref, h_ref, a_ref
):
    first, _ = own_bits()
    h_ref[:T, :] = right1_ref[:T, :]
    h_ref[T:, :] = right2_ref[:T, :]
    a_ref[:T, :] = right1_ref[T:, :]
    a_ref[T:, :] = right2_ref[T:, :]
    for p, out_ref in enumerate((out0_ref, out1_ref, out2_ref)):
        for i in range(4):
            bits = [None] * 3
            bits[p] = first[p] ^ flip
            bits[(p + 1) % 3] = i >> 1
            bits[(p + 2) % 3] = i & 1
            j = 4 * bits[0] + 2 * bits[1] + bits[2]
            rows = slice(i * Q_PAD, (i + 1) * Q_PAD)
            ql_ref[rows, :T] = left1_ref[j, :Q_PAD]
            ql_ref[rows, T:] = left2_ref[j, :Q_PAD]
            rows = slice(i * P_PAD, (i + 1) * P_PAD)
            pl_ref[rows, :T] = left1_ref[j, Q_PAD:]
            pl_ref[rows, T:] = left2_ref[j, Q_PAD:]
        cols = slice(p * PART, (p + 1) * PART)
        q = dot(ql_ref[...], h_ref[:, cols])
        o = dot(pl_ref[...], a_ref[:, cols])
        for i in range(4):
            out_ref[i] = jnp.concatenate(
                [q[i * Q_PAD : i * Q_PAD + Q_CHUNK], o[i * P_PAD : i * P_PAD + P_CHUNK]], axis=0
            ).astype(bf16)


def spatial_attention_back_kernel(
    gm_ref, mod_ref, inv_ref, kept_hbm, raw_hbm, w_hbm, grad_ref,
    w_ref, go_ref, g_ref, kept_ref, raw_ref, sems, in_sems,
):
    copies = weight_copies(w_hbm, w_ref, sems, range(QKV_CHUNKS, W_CHUNKS))
    kept = [
        pltpu.make_async_copy(kept_hbm.at[pl.ds(0, 4 * HEADS)], kept_ref, in_sems.at[0]),
        pltpu.make_async_copy(raw_hbm.at[pl.ds(0, HEADS)], raw_ref, in_sems.at[1]),
    ]
    for c in copies + kept:
        c.start()
    gm = gm_ref[...].astype(f32).reshape(T, D)
    go_ref[...] = (gm * mod_ref[2:3, :]).astype(bf16)
    for c in copies:
        c.wait()
    grad_heads(w_ref[...], go_ref[...], g_ref)
    for c in kept:
        c.wait()

    def group(i, _):
        heads = [i * GROUP + s for s in range(GROUP)]
        scaled, grad_probs, inners = [], [], []
        for h in heads:
            g = (g_ref[h].astype(f32) * inv_ref[h]).astype(bf16)
            scaled.append(g)
            out = kept_ref[3 * HEADS + h, :HEAD].astype(f32)
            inners.append(jnp.sum(g.astype(f32) * out, axis=0, keepdims=True))
            grad_probs.append(dot(kept_ref[2 * HEADS + h, :HEAD], g, TN))
        for h, g, inner, gp in zip(heads, scaled, inners, grad_probs):
            raw = raw_ref[h]
            grad_score = (raw.astype(f32) * (gp - inner)).astype(bf16)
            dq, dk = score_grads(kept_ref[h, :HEAD], kept_ref[HEADS + h, :HEAD], grad_score)
            for n, value in enumerate((dq, dk, dot(g, raw, NT))):
                grad_ref[n * HEADS + h] = value.astype(bf16)
        return _

    lax.fori_loop(0, HEADS // GROUP, group, 0)


def spatial_norm_back_kernel(
    grad_ref, gm_in, x_ref, mod_ref, w_hbm, out_ref, w_ref, cat_ref, gh_ref, gm_ref, sems
):
    copies = weight_copies(w_hbm, w_ref, sems, range(QKV_CHUNKS))
    start_weights(copies)
    gm_ref[...] = gm_in[...].astype(f32).reshape(T, D).astype(bf16)
    for h in range(0, 3 * HEADS, 2):
        pair = jnp.concatenate([grad_ref[h].astype(f32), grad_ref[h + 1].astype(f32)], axis=0)
        cat_ref[h * HEAD : (h + 2) * HEAD, :] = pair.astype(bf16)
    flipped = cat_ref[...].T
    for n in range(3):
        for i in range(QKV_CHUNKS // 3):
            next_weights(copies, n * (QKV_CHUNKS // 3) + i)
        cols = slice(n * D, (n + 1) * D)
        part = dot(flipped[:, cols], w_ref[cols, :])
        gh_ref[...] = part if n == 0 else gh_ref[...] + part
    norm_back_rows(x_ref, gm_ref, gh_ref, mod_ref, 1, out_ref)


def chunk_bits():
    first, _ = own_bits()
    return [(first[(p + 1) % 3], first[(p + 2) % 3]) for p in range(3)]


def second_send_kernel(*refs):
    keep, got, out = refs[0:3], refs[3:6], refs[7:10]
    for p, (a, _) in enumerate(chunk_bits()):
        for j in range(2):
            i = 2 * (1 - a) + j
            out[p][j] = (keep[p][i].astype(f32) + got[p][i].astype(f32)).astype(bf16)


def third_send_kernel(*refs):
    keep, got, more, out = refs[0:3], refs[3:6], refs[6:9], refs[10:13]
    for p, (a, b) in enumerate(chunk_bits()):
        i = 2 * a + 1 - b
        out[p][...] = (
            keep[p][i].astype(f32) + got[p][i].astype(f32) + more[p][1 - b].astype(f32)
        ).astype(bf16)


def xor_pairs(flips):
    pairs = []
    for coord in all_coords():
        other = list(coord)
        for axis in range(2):
            if (flips >> (1 - axis)) & 1:
                other[axis] = GRAY.index(GRAY[coord[axis]] ^ (1 << (1 - coord[3])))
        pairs.append((device_index(*coord), device_index(*other)))
    return pairs


def split_rows(total_ref, count, part_ref):
    rows = total_ref.shape[0]
    q_rows = rows * Q_ROWS // (Q_ROWS + P_ROWS) // count
    p_rows = rows // count - q_rows
    for k in range(count):
        p = count * q_rows + k * p_rows
        part_ref[k, :q_rows] = total_ref[k * q_rows : (k + 1) * q_rows, :]
        part_ref[k, q_rows:] = total_ref[p : p + p_rows, :]


def fourth_send_kernel(*refs):
    keep, got, more, most = refs[0:3], refs[3:6], refs[6:9], refs[9:12]
    own_ref, sends, row_ref, part_ref = refs[12], refs[13:16], refs[16], refs[17]
    for p, (a, b) in enumerate(chunk_bits()):
        i = 2 * a + b
        row_ref[:, p * PART : (p + 1) * PART] = (
            keep[p][i].astype(f32) + got[p][i].astype(f32) + more[p][b].astype(f32)
        ) + most[p][...].astype(f32)
    split_rows(row_ref, 4, part_ref)
    _, last = own_bits()
    me = 2 * last[0] + last[1]
    own_ref[...] = part_ref[me]
    for d in range(1, 4):
        sends[d - 1][...] = part_ref[me ^ d].astype(bf16)


def fifth_send_kernel(own_in, got1_ref, got2_ref, got3_ref, own_ref, send_ref, row_ref, part_ref):
    row_ref[...] = (own_in[...] + got1_ref[...].astype(f32)) + (
        got2_ref[...].astype(f32) + got3_ref[...].astype(f32)
    )
    split_rows(row_ref, 2, part_ref)
    _, last = own_bits()
    own_ref[...] = part_ref[last[2]]
    send_ref[...] = part_ref[1 - last[2]].astype(bf16)


def last_sum_kernel(own_ref, got_ref, q_ref, p_ref):
    total = own_ref[...] + got_ref[...].astype(f32)
    q_ref[...] = total[:Q_ROWS]
    p_ref[...] = total[Q_ROWS:]


VMEM = pl.BlockSpec(memory_space=pltpu.VMEM)
ANY = pl.BlockSpec(memory_space=pl.ANY)


def call(kernel, outs, scratch, specs, flops, name, out_specs=None, limit=54):
    return pl.pallas_call(
        kernel,
        out_shape=[jax.ShapeDtypeStruct(s, d) for s, d in outs],
        in_specs=specs,
        out_specs=out_specs or [VMEM] * len(outs),
        scratch_shapes=scratch,
        compiler_params=pltpu.CompilerParams(vmem_limit_bytes=limit * 1024 * 1024),
        cost_estimate=pl.CostEstimate(flops=flops, bytes_accessed=12_000_000 if flops > 1_000_000_000 else 1_000, transcendentals=0),
        name=name,
    )


WEIGHT = pltpu.VMEM((4 * D, D), bf16)
W_QKV = pltpu.VMEM((3 * D, D), bf16)
W_OUT = pltpu.VMEM((D, D), bf16)
SEMS = pltpu.SemaphoreType.DMA((W_CHUNKS,))
QK = ((2 * HEADS, V_ROWS, T), bf16)
V = ((HEADS, V_ROWS, T), bf16)
HEAD_ROWS = ((HEADS, HEAD, T), bf16)
TOKENS = ((T, D), bf16)


RAW = ((HEADS, T, T), bf16)


def spatial_forward(x, cot, mod, w):
    return call(
        spatial_forward_kernel,
        [((FRAMES, 2 * PLACE, D), bf16), KEPT, KEPT_RAW, ((HEADS, 1, T), f32)],
        [
            WEIGHT,
            pltpu.VMEM(*TOKENS),
            pltpu.VMEM((D, T), f32),
            pltpu.VMEM(*QK),
            pltpu.VMEM(*V),
            pltpu.VMEM(*V),
            pltpu.VMEM(*RAW),
            SEMS,
            pltpu.SemaphoreType.DMA((3 + HEADS // GROUP,)),
        ],
        [VMEM, VMEM, VMEM, ANY],
        6_000_000_000,
        "spatial_forward",
        [VMEM, ANY, ANY, VMEM],
    )(x, cot, mod, w)


LEFT = ((SUBS, Q_PAD + P_PAD, T), bf16)
RIGHT = ((2 * T, D), bf16)


def temporal(both, mod, w):
    return call(
        temporal_kernel,
        [((FRAMES, PLACE, D), bf16), RIGHT, LEFT, LEFT],
        [
            WEIGHT,
            pltpu.VMEM(*TOKENS),
            pltpu.VMEM(*TOKENS),
            pltpu.VMEM(*TOKENS),
            pltpu.VMEM(*TOKENS),
            pltpu.VMEM(*QK),
            pltpu.VMEM(*HEAD_ROWS),
            pltpu.VMEM(*HEAD_ROWS),
            pltpu.VMEM((D, T), f32),
            pltpu.VMEM((3 * D, T), f32),
            pltpu.VMEM((T, D), f32),
            pltpu.VMEM((2, Q_PAD, T), f32),
            pltpu.VMEM((2, P_PAD, T), f32),
            SEMS,
        ],
        [VMEM, VMEM, ANY],
        12_000_000_000,
        "temporal_sublayer",
    )(both, mod, w)


def weight_grad(flip, *operands):
    return call(
        functools.partial(weight_grad_kernel, flip),
        [((4, CHUNK, PART), bf16)] * 3,
        [
            pltpu.VMEM((4 * Q_PAD, 2 * T), bf16),
            pltpu.VMEM((4 * P_PAD, 2 * T), bf16),
            pltpu.VMEM((2 * T, D), bf16),
            pltpu.VMEM((2 * T, D), bf16),
        ],
        [VMEM] * 4,
        10_000_000,
        "weight_grad_send" if flip else "weight_grad_keep",
        limit=20,
    )(*operands)


def spatial_attention_back(gm, mod, kept, raw, inv, w):
    return call(
        spatial_attention_back_kernel,
        [((3 * HEADS, HEAD, T), bf16)],
        [
            W_OUT,
            pltpu.VMEM(*TOKENS),
            pltpu.VMEM(*HEAD_ROWS),
            pltpu.VMEM((4 * HEADS, V_ROWS, T), bf16),
            pltpu.VMEM(*RAW),
            SEMS,
            pltpu.SemaphoreType.DMA((2,)),
        ],
        [VMEM] * 3 + [ANY] * 3,
        5_000_000_000,
        "spatial_attention_back",
    )(gm, mod, inv, kept, raw, w)[0]


def spatial_norm_back(grad, gm, x, mod, w):
    return call(
        spatial_norm_back_kernel,
        [TOKENS],
        [W_QKV, pltpu.VMEM((3 * D, T), bf16), pltpu.VMEM((T, D), f32), pltpu.VMEM(*TOKENS), SEMS],
        [VMEM] * 4 + [ANY],
        5_000_000_000,
        "spatial_norm_back",
    )(grad, gm, x, mod, w)[0]


def reduce_rows(send, keep, before_second, before_third):
    half, one = ((2, CHUNK, PART), bf16), ((CHUNK, PART), bf16)
    got = [lax.ppermute(send[p], BOTH, flip_pairs(p, (0, 1))) for p in range(3)]
    out = call(second_send_kernel, [half] * 3, [], [VMEM] * 6 + [ANY], 1_000_000, "second_send", limit=12)(
        *keep, *got, before_second
    )
    more = [lax.ppermute(out[p], BOTH, flip_pairs((p + 1) % 3, (0, 1))) for p in range(3)]
    out = call(third_send_kernel, [one] * 3, [], [VMEM] * 9 + [ANY], 1_000_000, "third_send", limit=12)(
        *keep, *got, *more, before_third
    )
    most = [lax.ppermute(out[p], BOTH, flip_pairs((p + 2) % 3, (0, 1))) for p in range(3)]
    rows = CHUNK // 4
    own, *out = call(
        fourth_send_kernel,
        [((rows, D), f32)] + [((rows, D), bf16)] * 3,
        [pltpu.VMEM((CHUNK, D), f32), pltpu.VMEM((4, rows, D), f32)],
        [VMEM] * 12,
        1_000_000,
        "fourth_send",
        limit=16,
    )(*keep, *got, *more, *most)
    moved = [lax.ppermute(out[d - 1], BOTH, xor_pairs(d)) for d in range(1, 4)]
    own, sent = call(
        fifth_send_kernel,
        [((rows // 2, D), f32), ((rows // 2, D), bf16)],
        [pltpu.VMEM((rows, D), f32), pltpu.VMEM((2, rows // 2, D), f32)],
        [VMEM] * 4,
        1_000_000,
        "fifth_send",
        limit=8,
    )(own, *moved)
    moved = lax.ppermute(sent, BOTH, flip_pairs(2, (1, 0)))
    return call(
        last_sum_kernel,
        [((Q_ROWS, D), f32), ((P_ROWS, D), f32)],
        [],
        [VMEM] * 2,
        1_000_000,
        "last_sum",
        limit=8,
    )(own, moved)


def on_device(clip_tokens, modulation, spatial_weights, temporal_weights, out_cotangent):
    x = clip_tokens.reshape(T, D)
    cot = out_cotangent.reshape(T, D)
    mod = modulation.reshape(6, D)
    both, kept, raw, inv = spatial_forward(x, cot, mod, spatial_weights)
    both_pos = lax.all_to_all(both, "seq", 0, 0, tiled=True)
    gm_pos, right, left, theirs = temporal(both_pos, mod, temporal_weights)
    gm = lax.all_to_all(gm_pos, "seq", 0, 0, tiled=True)
    operands = (left, lax.ppermute(theirs, BOTH, core_pairs()), right, lax.ppermute(right, BOTH, core_pairs()))
    send = weight_grad(1, *operands)
    keep = weight_grad(0, *operands)
    grad = spatial_attention_back(gm, mod, kept, raw, inv, spatial_weights)
    input_grad = spatial_norm_back(grad, gm, x, mod, spatial_weights)
    qkv_rows, proj_rows = reduce_rows(send, keep, grad, input_grad)
    return input_grad.reshape(clip_tokens.shape), qkv_rows, proj_rows


def solution(mesh):
    placed = (
        P("rep", "seq", None, None),
        P("rep", None, None),
        P(),
        P(),
        P("rep", "seq", None, None),
    )
    return jax.shard_map(
        on_device,
        mesh=mesh,
        in_specs=placed,
        out_specs=(P("rep", "seq", None, None), P(BOTH, None), P(BOTH, None)),
        check_vma=False,
    )
```

```python
import functools

import jax
import jax.numpy as jnp
import numpy as np
from jax import lax
from jax.experimental import pallas as pl
from jax.experimental.pallas import tpu as pltpu
from jax.sharding import PartitionSpec as P

HEADS = 16
HEAD = 72
D = HEADS * HEAD
T = 256
PLACE = 4
FACTOR = HEAD**-0.5
LOG2E = 1.4426950408889634
BOTH = ("seq", "rep")
Q_ROWS = 27
P_ROWS = 9
SUBS = 8
Q_CHUNK = SUBS * Q_ROWS
P_CHUNK = SUBS * P_ROWS
CHUNK = Q_CHUNK + P_CHUNK
Q_PAD = 224
P_PAD = 80
KEPT = ((280, 80, 256), jnp.bfloat16)
KEPT_RAW = ((88, 256, 256), jnp.bfloat16)
KEPT_SUMS = ((200, 288, 384), jnp.bfloat16)
GROUP = 4
V_ROWS = 80
FRAMES = 64
PART = 384
bf16 = jnp.bfloat16
f32 = jnp.float32

NN = (((1,), (0,)), ((), ()))
NT = (((1,), (1,)), ((), ()))
TN = (((0,), (0,)), ((), ()))


def dot(a, b, dims=NN):
    return lax.dot_general(a, b, dims, preferred_element_type=f32)


GRAY = (0, 1, 3, 2)


def device_index(x, y, z, core):
    return ((((x % 2) * 4 + z) * 4 + y) * 2 + core) * 2 + x // 2


def all_coords():
    return [
        (x, y, z, core)
        for x in range(4)
        for y in range(4)
        for z in range(4)
        for core in range(2)
    ]


def flip_pairs(axis, bits):
    pairs = []
    for coord in all_coords():
        other = list(coord)
        other[axis] = GRAY.index(GRAY[coord[axis]] ^ (1 << bits[coord[3]]))
        pairs.append((device_index(*coord), device_index(*other)))
    return pairs


def core_pairs():
    return [(device_index(x, y, z, c), device_index(x, y, z, 1 - c)) for x, y, z, c in all_coords()]


def owner_of(core, chunk, sub):
    coord = []
    for axis in range(3):
        high, low = (chunk >> (2 - axis)) & 1, (sub >> (2 - axis)) & 1
        code = (low << 1) | high if core == 0 else (high << 1) | low
        coord.append(GRAY.index(code))
    return device_index(*coord, core)


def normalize(tokens):
    values = tokens.astype(f32)
    center = values - jnp.mean(values, axis=-1, keepdims=True)
    spread = lax.rsqrt(jnp.mean(center * center, axis=-1, keepdims=True) + 1e-06)
    return center * spread, spread


ROWS = 64


def row(mod_ref, i):
    return mod_ref[i]


def modulated(src_ref, mod_ref, shift, scale, out_ref):
    for r in range(0, T, ROWS):
        normed, _ = normalize(src_ref[r : r + ROWS, :])
        out_ref[r : r + ROWS, :] = (
            normed * (1.0 + row(mod_ref, scale)) + row(mod_ref, shift)
        ).astype(bf16)


def norm_back_rows(src_ref, direct_ref, grad_ref, mod_ref, scale, out_ref):
    for r in range(0, T, ROWS):
        normed, spread = normalize(src_ref[r : r + ROWS, :])
        g = grad_ref[r : r + ROWS, :] * (1.0 + row(mod_ref, scale))
        centered = g - jnp.mean(g, axis=-1, keepdims=True)
        back = spread * (centered - normed * jnp.mean(g * normed, axis=-1, keepdims=True))
        out_ref[r : r + ROWS, :] = (direct_ref[r : r + ROWS, :].astype(f32) + back).astype(bf16)


W_ROWS = 1152
W_CHUNKS = 4 * D // W_ROWS
QKV_CHUNKS = 3 * D // W_ROWS


def weight_copies(w_hbm, w_ref, sems, chunks):
    return [
        pltpu.make_async_copy(
            w_hbm.at[pl.ds(i * W_ROWS, W_ROWS), :],
            w_ref.at[pl.ds((i - chunks[0]) * W_ROWS, W_ROWS), :],
            sems.at[i],
        )
        for i in chunks
    ]


SIDE = HEADS // 2 * HEAD


def qkv_heads(side, w_ref, hid_ref, qk_ref, v_ref):
    for n in range(3):
        start = n * D + side * SIDE
        block = dot(w_ref[start : start + SIDE, :], hid_ref[...], NT)
        for j in range(HEADS // 2):
            h = side * (HEADS // 2) + j
            rows = block[j * HEAD : (j + 1) * HEAD, :]
            if n == 0:
                qk_ref[h, :HEAD] = (rows * (FACTOR * LOG2E)).astype(bf16)
            elif n == 1:
                qk_ref[HEADS + h, :HEAD] = rows.astype(bf16)
            else:
                v_ref[h, :HEAD] = rows.astype(bf16)


def score_grads(q, k, grad_score):
    return dot(k, grad_score) * FACTOR, dot(q, grad_score, NT) * (1.0 / LOG2E)


def grad_heads(w, go, out_ref):
    block = dot(go, w).T
    for h in range(HEADS):
        out_ref[h] = block[h * HEAD : (h + 1) * HEAD, :].astype(bf16)


def spatial_forward_kernel(
    x_ref, cot_hbm, mod_ref, w_hbm,
    both_ref, kept_out, raw_out, inv_ref,
    w_ref, cot_ref, hid_ref, attn_ref, qk_ref, v_ref, o_ref, raw_ref, sems, out_sems,
):
    blocks_of = [(n * D + side * SIDE, SIDE) for side in range(2) for n in range(3)] + [(3 * D, D)]
    copies = [
        pltpu.make_async_copy(w_hbm.at[pl.ds(r, size), :], w_ref.at[pl.ds(r, size), :], sems.at[i])
        for i, (r, size) in enumerate(blocks_of)
    ]
    copies.append(pltpu.make_async_copy(cot_hbm, cot_ref, sems.at[7]))
    for c in copies:
        c.start()
    v_ref[:, HEAD:V_ROWS, :] = jnp.ones((HEADS, V_ROWS - HEAD, T), bf16)
    modulated(x_ref, mod_ref, 0, 1, hid_ref)
    def raw_copy(i):
        part = pl.ds(i * GROUP, GROUP)
        return pltpu.make_async_copy(raw_ref.at[part], raw_out.at[part], out_sems.at[3 + i])

    def group(i, _):
        heads = [i * GROUP + s for s in range(GROUP)]
        scores = [dot(qk_ref[HEADS + h, :HEAD], qk_ref[h, :HEAD], TN) for h in heads]
        raws = []
        for h, sc in zip(heads, scores):
            raws.append(jnp.exp2(sc - jnp.max(sc, axis=0, keepdims=True)).astype(bf16))
            raw_ref[h] = raws[-1]
        raw_copy(i).start()
        for h, raw in zip(heads, raws):
            mixed = dot(v_ref[h], raw)
            inv = 1.0 / mixed[HEAD : HEAD + 1]
            inv_ref[h] = inv
            out = mixed[:HEAD] * inv
            o_ref[h, :HEAD] = out.astype(bf16)
            attn_ref[pl.ds(pl.multiple_of(h * HEAD, 8), HEAD), :] = out
        return _

    for side in range(2):
        for c in copies[3 * side : 3 * side + 3]:
            c.wait()
        qkv_heads(side, w_ref, hid_ref, qk_ref, v_ref)
        lax.fori_loop(side * HEADS // GROUP // 2, (side + 1) * HEADS // GROUP // 2, group, 0)
    kept = [
        pltpu.make_async_copy(qk_ref, kept_out.at[pl.ds(0, 2 * HEADS)], out_sems.at[0]),
        pltpu.make_async_copy(v_ref, kept_out.at[pl.ds(2 * HEADS, HEADS)], out_sems.at[1]),
    ]
    for c in kept:
        c.start()
    kept.append(pltpu.make_async_copy(o_ref, kept_out.at[pl.ds(3 * HEADS, HEADS)], out_sems.at[2]))
    kept[-1].start()
    copies[6].wait()
    copies[7].wait()
    both_ref[:, PLACE:, :] = cot_ref[...].astype(f32).reshape(FRAMES, PLACE, D).astype(bf16)
    block = dot(w_ref[3 * D :, :], attn_ref[...].astype(bf16)).T
    middle = x_ref[...].astype(f32) + row(mod_ref, 2) * block
    both_ref[:, :PLACE, :] = middle.reshape(FRAMES, PLACE, D).astype(bf16)
    for c in kept + [raw_copy(i) for i in range(HEADS // GROUP)]:
        c.wait()


def gather_rows(src_ref, tmp_ref, mine_ref, theirs_ref, rows, start):
    me = lax.axis_index("seq") % 2
    padded = tmp_ref.shape[1]
    tmp_ref[...] = jnp.zeros_like(tmp_ref)
    for core in range(2):
        for chunk in range(SUBS):
            slot = (core * SUBS + chunk) % 2
            for sub in range(SUBS):
                first = rows * owner_of(core, chunk, sub)
                tmp_ref[slot, rows * sub : rows * (sub + 1), :] = src_ref[first : first + rows, :]
            low = tmp_ref[slot].astype(bf16)

            @pl.when(me == core)
            def _(chunk=chunk, low=low):
                mine_ref[chunk, start : start + padded] = low

            @pl.when(me != core)
            def _(chunk=chunk, low=low):
                theirs_ref[chunk, start : start + padded] = low


def by_position(both, start):
    row = lax.broadcasted_iota(jnp.int32, (T, 2 * T), 0)
    col = lax.broadcasted_iota(jnp.int32, (T, 2 * T), 1)
    source = (row % FRAMES) * (2 * PLACE) + row // FRAMES + start
    return dot(jnp.where(source == col, 1.0, 0.0).astype(bf16), both).astype(bf16)


def by_frame(tokens):
    row = lax.broadcasted_iota(jnp.int32, (T, T), 0)
    col = lax.broadcasted_iota(jnp.int32, (T, T), 1)
    source = (row % PLACE) * FRAMES + row // PLACE
    return dot(jnp.where(source == col, 1.0, 0.0).astype(bf16), tokens)


def temporal_kernel(
    both_hbm, mod_ref, w_hbm,
    gm_out, right_ref, mine_ref, theirs_ref,
    w_ref, both_ref, m_ref, cot_ref, gm_ref, hid_ref, qk_ref, v_ref, g_ref, attn_ref, grad_ref, gh_ref,
    tmp_ref, tmp_p_ref, sems,
):
    first = pltpu.make_async_copy(both_hbm, both_ref, sems.at[0])
    weights = pltpu.make_async_copy(w_hbm, w_ref, sems.at[1])
    first.start()
    weights.start()
    first.wait()
    both = both_ref[...].reshape(2 * T, D)
    m_ref[...] = by_position(both, 0)
    modulated(m_ref, mod_ref, 3, 4, hid_ref)
    right_ref[:T, :] = hid_ref[...]
    cot_ref[...] = by_position(both, PLACE)
    go = (cot_ref[...].astype(f32) * row(mod_ref, 5)).astype(bf16)
    grad_ref[:D, :] = go.astype(f32).T
    gather_rows(grad_ref, tmp_p_ref, mine_ref, theirs_ref, P_ROWS, Q_PAD)
    weights.wait()
    for side in range(2):
        qkv_heads(side, w_ref, hid_ref, qk_ref, v_ref)
    grad_heads(w_ref[3 * D :, :], go, g_ref)

    def group(i, _):
        heads = [i * GROUP + s for s in range(GROUP)]
        scores = [blocks(dot(qk_ref[HEADS + h, :HEAD], qk_ref[h, :HEAD], TN)) for h in heads]
        raws = [jnp.exp2(sc - jnp.max(sc, axis=0, keepdims=True)) for sc in scores]
        probs = [raw * (1.0 / jnp.sum(raw, axis=0, keepdims=True)) for raw in raws]
        lows = [spread(prob) for prob in probs]
        grad_probs = [blocks(dot(v_ref[h], g_ref[h], TN)) for h in heads]
        for h, prob, low, gp in zip(heads, probs, lows, grad_probs):
            inner = jnp.sum(prob * gp, axis=0, keepdims=True)
            grad_score = spread(prob * (gp - inner))
            dq, dk = score_grads(qk_ref[h, :HEAD], qk_ref[HEADS + h, :HEAD], grad_score)
            dv = dot(g_ref[h], low, NT)
            attn_ref[pl.ds(pl.multiple_of(h * HEAD, 8), HEAD), :] = dot(v_ref[h], low)
            for n, value in enumerate((dq, dk, dv)):
                grad_ref[pl.ds(pl.multiple_of(n * D + h * HEAD, 8), HEAD), :] = value
        return _

    lax.fori_loop(0, HEADS // GROUP, group, 0)
    gh_ref[...] = dot(grad_ref[...].astype(bf16).T, w_ref[: 3 * D, :])
    norm_back_rows(m_ref, cot_ref, gh_ref, mod_ref, 4, gm_ref)
    gm_out[...] = by_frame(gm_ref[...]).reshape(FRAMES, PLACE, D).astype(bf16)
    right_ref[T:, :] = attn_ref[...].astype(bf16).T
    gather_rows(grad_ref, tmp_ref, mine_ref, theirs_ref, Q_ROWS, 0)


def first_lanes():
    return lax.broadcasted_iota(jnp.int32, (FRAMES, 2 * FRAMES), 1) < FRAMES


def blocks(full):
    f, lane = FRAMES, first_lanes()
    left = jnp.where(lane, full[:f, : 2 * f], full[f : 2 * f, : 2 * f])
    right = jnp.where(lane, full[2 * f : 3 * f, 2 * f :], full[3 * f :, 2 * f :])
    return jnp.concatenate([left, right], axis=1)


def spread(side):
    lane = first_lanes()
    zero = jnp.zeros((FRAMES, 2 * FRAMES), f32)
    a, b = side[:, : 2 * FRAMES], side[:, 2 * FRAMES :]
    left = jnp.concatenate([jnp.where(lane, a, zero), jnp.where(lane, zero, a), zero, zero], axis=0)
    right = jnp.concatenate([zero, zero, jnp.where(lane, b, zero), jnp.where(lane, zero, b)], axis=0)
    return jnp.concatenate([left, right], axis=1).astype(bf16)


def own_bits():
    seq, rep = lax.axis_index("seq"), lax.axis_index("rep")
    core = seq % 2
    ring = (rep * 2 + seq // 32, (seq // 2) % 4, (seq // 8) % 4)
    codes = [v ^ (v >> 1) for v in ring]
    first = [jnp.where(core == 0, v & 1, v >> 1) for v in codes]
    last = [jnp.where(core == 0, v >> 1, v & 1) for v in codes]
    return first, last


def weight_grad_kernel(
    flip, left1_ref, left2_ref, right1_ref, right2_ref, *refs
):
    if flip:
        out0_ref, out1_ref, out2_ref, token_ref, ql_ref, pl_ref, h_ref, a_ref = refs
        token_ref[...] = jnp.zeros_like(token_ref)
        moved = []
    else:
        gm_in, _, out_hbm, gm_out, ql_ref, pl_ref, h_ref, a_ref, out0_ref, out1_ref, out2_ref, sem, out_sems = refs
        passed = pltpu.make_async_copy(gm_in, gm_out, sem)
        passed.start()
        moved = [passed]
    first, _ = own_bits()
    h_ref[:T, :] = right1_ref[:T, :]
    h_ref[T:, :] = right2_ref[:T, :]
    a_ref[:T, :] = right1_ref[T:, :]
    a_ref[T:, :] = right2_ref[T:, :]
    for p, out_ref in enumerate((out0_ref, out1_ref, out2_ref)):
        for i in range(4):
            bits = [None] * 3
            bits[p] = first[p] ^ flip
            bits[(p + 1) % 3] = i >> 1
            bits[(p + 2) % 3] = i & 1
            j = 4 * bits[0] + 2 * bits[1] + bits[2]
            rows = slice(i * Q_PAD, (i + 1) * Q_PAD)
            ql_ref[rows, :T] = left1_ref[j, :Q_PAD]
            ql_ref[rows, T:] = left2_ref[j, :Q_PAD]
            rows = slice(i * P_PAD, (i + 1) * P_PAD)
            pl_ref[rows, :T] = left1_ref[j, Q_PAD:]
            pl_ref[rows, T:] = left2_ref[j, Q_PAD:]
        cols = slice(p * PART, (p + 1) * PART)
        q = dot(ql_ref[...], h_ref[:, cols])
        o = dot(pl_ref[...], a_ref[:, cols])
        for i in range(4):
            out_ref[i] = jnp.concatenate(
                [q[i * Q_PAD : i * Q_PAD + Q_CHUNK], o[i * P_PAD : i * P_PAD + P_CHUNK]], axis=0
            ).astype(bf16)
        if not flip:
            moved.append(pltpu.make_async_copy(out_ref, out_hbm.at[pl.ds(4 * p, 4)], out_sems.at[p]))
            moved[-1].start()
    for c in moved:
        c.wait()


HALF = HEADS // 2


def spatial_attention_back_kernel(
    gm_ref, mod_ref, inv_ref, kept_hbm, raw_hbm, w_hbm, grad_out, token_ref,
    w_ref, g_ref, kept_ref, raw_ref, grad_ref, sems, in_sems,
):
    (weights,) = weight_copies(w_hbm, w_ref, sems, range(QKV_CHUNKS, W_CHUNKS))
    kept = []
    for side in range(2):
        copies = []
        for n in range(4):
            part = pl.ds(n * HEADS + side * HALF, HALF)
            copies.append(pltpu.make_async_copy(kept_hbm.at[part], kept_ref.at[part], in_sems.at[side, n]))
        part = pl.ds(side * HALF, HALF)
        copies.append(pltpu.make_async_copy(raw_hbm.at[part], raw_ref.at[part], in_sems.at[side, 4]))
        kept.append(copies)
    for c in [weights] + kept[0]:
        c.start()
    token_ref[...] = jnp.zeros_like(token_ref)
    go = (gm_ref[...].astype(f32).reshape(T, D) * row(mod_ref, 2)).astype(bf16)
    weights.wait()
    for c in kept[1]:
        c.start()
    grad_heads(w_ref[...], go, g_ref)

    def group(i, _):
        heads = [i * GROUP + s for s in range(GROUP)]
        scaled, grad_probs, inners = [], [], []
        for h in heads:
            g = (g_ref[h].astype(f32) * inv_ref[h]).astype(bf16)
            scaled.append(g)
            out = kept_ref[3 * HEADS + h, :HEAD].astype(f32)
            inners.append(jnp.sum(g.astype(f32) * out, axis=0, keepdims=True))
            grad_probs.append(dot(kept_ref[2 * HEADS + h, :HEAD], g, TN))
        for h, g, inner, gp in zip(heads, scaled, inners, grad_probs):
            raw = raw_ref[h]
            grad_score = (raw.astype(f32) * (gp - inner)).astype(bf16)
            dq, dk = score_grads(kept_ref[h, :HEAD], kept_ref[HEADS + h, :HEAD], grad_score)
            for n, value in enumerate((dq, dk, dot(g, raw, NT))):
                grad_ref[pl.ds(pl.multiple_of(n * D + h * HEAD, 8), HEAD), :] = value
        return _

    for side in range(2):
        for c in kept[side]:
            c.wait()
        lax.fori_loop(side * HALF // GROUP, (side + 1) * HALF // GROUP, group, 0)
    grad_out[...] = grad_ref[...].astype(bf16)


def spatial_norm_back_kernel(
    grad_ref, gm_hbm, x_hbm, mod_ref, w_hbm, out_ref, token_ref, w_ref, gh_ref, gm_in, gm_ref, x_ref, sems, in_sems
):
    copies = weight_copies(w_hbm, w_ref, sems, range(QKV_CHUNKS))
    copies.append(pltpu.make_async_copy(gm_hbm, gm_in, in_sems.at[0]))
    copies.append(pltpu.make_async_copy(x_hbm, x_ref, in_sems.at[1]))
    for c in copies:
        c.start()
    token_ref[...] = jnp.zeros_like(token_ref)
    flipped = grad_ref[...].T
    copies[0].wait()
    copies[1].wait()
    gh_ref[...] = dot(flipped[:, : 2 * D], w_ref[: 2 * D, :])
    for c in copies[2:]:
        c.wait()
    gm_ref[...] = gm_in[...].astype(f32).reshape(T, D).astype(bf16)
    gh_ref[...] = gh_ref[...] + dot(flipped[:, 2 * D :], w_ref[2 * D :, :])
    norm_back_rows(x_ref, gm_ref, gh_ref, mod_ref, 1, out_ref)


def chunk_bits():
    first, _ = own_bits()
    return [(first[(p + 1) % 3], first[(p + 2) % 3]) for p in range(3)]


def second_sums_kernel(flip, *refs):
    keep_hbm, got, out, keep, sems = refs[0], refs[1:4], refs[4:7], refs[7:10], refs[10]
    bits = [a ^ flip for a, _ in chunk_bits()]
    copies = [
        pltpu.make_async_copy(keep_hbm.at[pl.ds(4 * p + 2 * a, 2)], keep[p], sems.at[p])
        for p, a in enumerate(bits)
    ]
    for c in copies:
        c.start()
    for p, a in enumerate(bits):
        copies[p].wait()
        for j in range(2):
            out[p][j] = (keep[p][j].astype(f32) + got[p][2 * a + j].astype(f32)).astype(bf16)


def third_send_kernel(*refs):
    keep, got, own, out = refs[0:3], refs[3:6], refs[6:9], refs[9:12]
    for p, (_, b) in enumerate(chunk_bits()):
        for to, i in ((out, 1 - b), (own, b)):
            to[p][...] = (keep[p][i].astype(f32) + got[p][i].astype(f32)).astype(bf16)


def xor_pairs(flips):
    pairs = []
    for coord in all_coords():
        other = list(coord)
        for axis in range(2):
            if (flips >> (1 - axis)) & 1:
                other[axis] = GRAY.index(GRAY[coord[axis]] ^ (1 << (1 - coord[3])))
        pairs.append((device_index(*coord), device_index(*other)))
    return pairs


def split_rows(total_ref, count, part_ref):
    rows = total_ref.shape[0]
    q_rows = rows * Q_ROWS // (Q_ROWS + P_ROWS) // count
    p_rows = rows // count - q_rows
    for k in range(count):
        p = count * q_rows + k * p_rows
        part_ref[k, :q_rows] = total_ref[k * q_rows : (k + 1) * q_rows, :]
        part_ref[k, q_rows:] = total_ref[p : p + p_rows, :]


def fourth_send_kernel(*refs):
    keep, got = refs[0:3], refs[3:6]
    own_ref, sends, row_ref, part_ref = refs[7], refs[8:11], refs[11], refs[12]
    for p in range(3):
        row_ref[:, p * PART : (p + 1) * PART] = keep[p][...].astype(f32) + got[p][...].astype(f32)
    split_rows(row_ref, 4, part_ref)
    _, last = own_bits()
    me = 2 * last[0] + last[1]
    own_ref[...] = part_ref[me]
    for d in range(1, 4):
        sends[d - 1][...] = part_ref[me ^ d].astype(bf16)


def fifth_send_kernel(own_in, got1_ref, got2_ref, got3_ref, _, own_ref, send_ref, row_ref, part_ref):
    row_ref[...] = (own_in[...] + got1_ref[...].astype(f32)) + (
        got2_ref[...].astype(f32) + got3_ref[...].astype(f32)
    )
    split_rows(row_ref, 2, part_ref)
    _, last = own_bits()
    own_ref[...] = part_ref[last[2]]
    send_ref[...] = part_ref[1 - last[2]].astype(bf16)


def last_sum_kernel(own_ref, got_ref, q_ref, p_ref):
    total = own_ref[...] + got_ref[...].astype(f32)
    q_ref[...] = total[:Q_ROWS]
    p_ref[...] = total[Q_ROWS:]


VMEM = pl.BlockSpec(memory_space=pltpu.VMEM)
ANY = pl.BlockSpec(memory_space=pl.ANY)


def call(kernel, outs, scratch, specs, flops, name, out_specs=None, limit=54):
    return pl.pallas_call(
        kernel,
        out_shape=[jax.ShapeDtypeStruct(s, d) for s, d in outs],
        in_specs=specs,
        out_specs=out_specs or [VMEM] * len(outs),
        scratch_shapes=scratch,
        compiler_params=pltpu.CompilerParams(vmem_limit_bytes=limit * 1024 * 1024),
        cost_estimate=pl.CostEstimate(flops=flops, bytes_accessed=12_000_000 if flops > 1_000_000_000 else 1_000, transcendentals=0),
        name=name,
    )


WEIGHT = pltpu.VMEM((4 * D, D), bf16)
TOKEN = ((8, 128), f32)
W_OUT = pltpu.VMEM((D, D), bf16)
SEMS = pltpu.SemaphoreType.DMA((W_CHUNKS,))
QK = ((2 * HEADS, V_ROWS, T), bf16)
V = ((HEADS, V_ROWS, T), bf16)
HEAD_ROWS = ((HEADS, HEAD, T), bf16)
TOKENS = ((T, D), bf16)


RAW = ((HEADS, T, T), bf16)


def spatial_forward(x, cot, mod, w):
    return call(
        spatial_forward_kernel,
        [((FRAMES, 2 * PLACE, D), bf16), KEPT, KEPT_RAW, ((HEADS, 1, T), f32)],
        [
            WEIGHT,
            pltpu.VMEM(*TOKENS),
            pltpu.VMEM(*TOKENS),
            pltpu.VMEM((D, T), f32),
            pltpu.VMEM(*QK),
            pltpu.VMEM(*V),
            pltpu.VMEM(*V),
            pltpu.VMEM(*RAW),
            pltpu.SemaphoreType.DMA((8,)),
            pltpu.SemaphoreType.DMA((3 + HEADS // GROUP,)),
        ],
        [VMEM, ANY, VMEM, ANY],
        6_000_000_000,
        "spatial_forward",
        [VMEM, ANY, ANY, VMEM],
    )(x, cot, mod, w)


LEFT = ((SUBS, Q_PAD + P_PAD, T), bf16)
RIGHT = ((2 * T, D), bf16)


def temporal(both, mod, w):
    return call(
        temporal_kernel,
        [((FRAMES, PLACE, D), bf16), RIGHT, LEFT, LEFT],
        [
            WEIGHT,
            pltpu.VMEM((FRAMES, 2 * PLACE, D), bf16),
            pltpu.VMEM(*TOKENS),
            pltpu.VMEM(*TOKENS),
            pltpu.VMEM(*TOKENS),
            pltpu.VMEM(*TOKENS),
            pltpu.VMEM(*QK),
            pltpu.VMEM(*HEAD_ROWS),
            pltpu.VMEM(*HEAD_ROWS),
            pltpu.VMEM((D, T), f32),
            pltpu.VMEM((3 * D, T), f32),
            pltpu.VMEM((T, D), f32),
            pltpu.VMEM((2, Q_PAD, T), f32),
            pltpu.VMEM((2, P_PAD, T), f32),
            pltpu.SemaphoreType.DMA((2,)),
        ],
        [ANY, VMEM, ANY],
        12_000_000_000,
        "temporal_sublayer",
        limit=40,
    )(both, mod, w)


def weight_grad(flip, *operands):
    part = ((4, CHUNK, PART), bf16)
    scratch = [
        pltpu.VMEM((4 * Q_PAD, 2 * T), bf16),
        pltpu.VMEM((4 * P_PAD, 2 * T), bf16),
        pltpu.VMEM((2 * T, D), bf16),
        pltpu.VMEM((2 * T, D), bf16),
    ]
    if not flip:
        scratch += [pltpu.VMEM(*part)] * 3 + [pltpu.SemaphoreType.DMA, pltpu.SemaphoreType.DMA((3,))]
    return call(
        functools.partial(weight_grad_kernel, flip),
        [part] * 3 + [TOKEN] if flip else [KEPT_SUMS, ((FRAMES, PLACE, D), bf16)],
        scratch,
        [VMEM] * 4 + [ANY] * (2 - 2 * flip),
        10_000_000,
        "weight_grad_send" if flip else "weight_grad_keep",
        [VMEM] * 4 if flip else [ANY] * 2,
        limit=20,
    )(*operands)


def spatial_attention_back(gm, mod, kept, raw, inv, w):
    return call(
        spatial_attention_back_kernel,
        [((3 * D, T), bf16), TOKEN],
        [
            W_OUT,
            pltpu.VMEM(*HEAD_ROWS),
            pltpu.VMEM((4 * HEADS, V_ROWS, T), bf16),
            pltpu.VMEM(*RAW),
            pltpu.VMEM((3 * D, T), f32),
            SEMS,
            pltpu.SemaphoreType.DMA((2, 5)),
        ],
        [VMEM] * 3 + [ANY] * 3,
        5_000_000_000,
        "spatial_attention_back",
    )(gm, mod, inv, kept, raw, w)


def spatial_norm_back(grad, gm, x, mod, w):
    return call(
        spatial_norm_back_kernel,
        [TOKENS, TOKEN],
        [
            pltpu.VMEM((3 * D, D), bf16),
            pltpu.VMEM((T, D), f32),
            pltpu.VMEM((FRAMES, PLACE, D), bf16),
            pltpu.VMEM(*TOKENS),
            pltpu.VMEM(*TOKENS),
            SEMS,
            pltpu.SemaphoreType.DMA((2,)),
        ],
        [VMEM, ANY, ANY, VMEM, ANY],
        5_000_000_000,
        "spatial_norm_back",
    )(grad, gm, x, mod, w)


def reduce_rows(send, keep, tokens):
    half, one = ((2, CHUNK, PART), bf16), ((CHUNK, PART), bf16)

    def second_sums(flip):
        return call(
            functools.partial(second_sums_kernel, flip),
            [half] * 3,
            [pltpu.VMEM(*half)] * 3 + [pltpu.SemaphoreType.DMA((3,))],
            [ANY] + [VMEM] * 3,
            1_000_000,
            "second_sums_send" if flip else "second_sums_own",
            limit=16,
        )(keep, *got)

    got = [lax.ppermute(send[p], BOTH, flip_pairs(p, (0, 1))) for p in range(3)]
    out, own = second_sums(1), second_sums(0)
    got = [lax.ppermute(out[p], BOTH, flip_pairs((p + 1) % 3, (0, 1))) for p in range(3)]
    outs = call(third_send_kernel, [one] * 6, [], [VMEM] * 6, 1_000_000, "third_send", limit=12)(*own, *got)
    own, out = outs[:3], outs[3:]
    got = [lax.ppermute(out[p], BOTH, flip_pairs((p + 2) % 3, (0, 1))) for p in range(3)]
    rows = CHUNK // 4
    own, *out = call(
        fourth_send_kernel,
        [((rows, D), f32)] + [((rows, D), bf16)] * 3,
        [pltpu.VMEM((CHUNK, D), f32), pltpu.VMEM((4, rows, D), f32)],
        [VMEM] * 6 + [ANY],
        1_000_000,
        "fourth_send",
        limit=16,
    )(*own, *got, tokens[0])
    moved = [lax.ppermute(out[d - 1], BOTH, xor_pairs(d)) for d in range(1, 4)]
    own, sent = call(
        fifth_send_kernel,
        [((rows // 2, D), f32), ((rows // 2, D), bf16)],
        [pltpu.VMEM((rows, D), f32), pltpu.VMEM((2, rows // 2, D), f32)],
        [VMEM] * 4 + [ANY],
        1_000_000,
        "fifth_send",
        limit=8,
    )(own, *moved, tokens[1])
    moved = lax.ppermute(sent, BOTH, flip_pairs(2, (1, 0)))
    return call(
        last_sum_kernel,
        [((Q_ROWS, D), f32), ((P_ROWS, D), f32)],
        [],
        [VMEM] * 2,
        1_000_000,
        "last_sum",
        limit=8,
    )(own, moved)


def on_device(clip_tokens, modulation, spatial_weights, temporal_weights, out_cotangent):
    x = clip_tokens.reshape(T, D)
    cot = out_cotangent.reshape(T, D)
    mod = modulation.reshape(6, 1, D)
    both, kept, raw, inv = spatial_forward(x, cot, mod, spatial_weights)
    both_pos = lax.all_to_all(both, "seq", 0, 0, tiled=True)
    gm_pos, right, left, theirs = temporal(both_pos, mod, temporal_weights)
    operands = (left, lax.ppermute(theirs, BOTH, core_pairs()), right, lax.ppermute(right, BOTH, core_pairs()))
    *send, token = weight_grad(1, *operands)
    keep, gm_pos = weight_grad(0, *operands, gm_pos, token)
    gm = lax.all_to_all(gm_pos, "seq", 0, 0, tiled=True)
    grad, token1 = spatial_attention_back(gm, mod, kept, raw, inv, spatial_weights)
    input_grad, token2 = spatial_norm_back(grad, gm, x, mod, spatial_weights)
    tokens = (token1, token2)
    qkv_rows, proj_rows = reduce_rows(send, keep, tokens)
    return input_grad.reshape(clip_tokens.shape), qkv_rows, proj_rows


def solution(mesh):
    placed = (
        P("rep", "seq", None, None),
        P("rep", None, None),
        P(),
        P(),
        P("rep", "seq", None, None),
    )
    return jax.shard_map(
        on_device,
        mesh=mesh,
        in_specs=placed,
        out_specs=(P("rep", "seq", None, None), P(BOTH, None), P(BOTH, None)),
        check_vma=False,
    )
```

```python
import functools

import jax
import jax.numpy as jnp
import numpy as np
from jax import lax
from jax.experimental import pallas as pl
from jax.experimental.pallas import tpu as pltpu
from jax.sharding import PartitionSpec as P

HEADS = 16
HEAD = 72
D = HEADS * HEAD
T = 256
PLACE = 4
FACTOR = HEAD**-0.5
LOG2E = 1.4426950408889634
BOTH = ("seq", "rep")
Q_ROWS = 27
P_ROWS = 9
SUBS = 8
Q_CHUNK = SUBS * Q_ROWS
P_CHUNK = SUBS * P_ROWS
CHUNK = Q_CHUNK + P_CHUNK
Q_PAD = 224
P_PAD = 80
KEPT = ((280, 80, 256), jnp.bfloat16)
KEPT_RAW = ((88, 256, 256), jnp.bfloat16)
KEPT_SUMS = ((200, 288, 384), jnp.bfloat16)
GROUP = 4
V_ROWS = 80
FRAMES = 64
PART = 384
bf16 = jnp.bfloat16
f32 = jnp.float32

NN = (((1,), (0,)), ((), ()))
NT = (((1,), (1,)), ((), ()))
TN = (((0,), (0,)), ((), ()))


def dot(a, b, dims=NN):
    return lax.dot_general(a, b, dims, preferred_element_type=f32)


GRAY = (0, 1, 3, 2)


def device_index(x, y, z, core):
    return ((((x % 2) * 4 + z) * 4 + y) * 2 + core) * 2 + x // 2


def all_coords():
    return [
        (x, y, z, core)
        for x in range(4)
        for y in range(4)
        for z in range(4)
        for core in range(2)
    ]


def flip_pairs(axis, bits):
    pairs = []
    for coord in all_coords():
        other = list(coord)
        other[axis] = GRAY.index(GRAY[coord[axis]] ^ (1 << bits[coord[3]]))
        pairs.append((device_index(*coord), device_index(*other)))
    return pairs


def core_pairs():
    return [(device_index(x, y, z, c), device_index(x, y, z, 1 - c)) for x, y, z, c in all_coords()]


def owner_of(core, chunk, sub):
    coord = []
    for axis in range(3):
        high, low = (chunk >> (2 - axis)) & 1, (sub >> (2 - axis)) & 1
        code = (low << 1) | high if core == 0 else (high << 1) | low
        coord.append(GRAY.index(code))
    return device_index(*coord, core)


def normalize(tokens):
    values = tokens.astype(f32)
    center = values - jnp.mean(values, axis=-1, keepdims=True)
    spread = lax.rsqrt(jnp.mean(center * center, axis=-1, keepdims=True) + 1e-06)
    return center * spread, spread


ROWS = 64


def row(mod_ref, i):
    return mod_ref[i]


def modulated(src_ref, mod_ref, shift, scale, out_ref):
    for r in range(0, T, ROWS):
        normed, _ = normalize(src_ref[r : r + ROWS, :])
        out_ref[r : r + ROWS, :] = (
            normed * (1.0 + row(mod_ref, scale)) + row(mod_ref, shift)
        ).astype(bf16)


def norm_back_rows(src_ref, direct_ref, grad_ref, mod_ref, scale, out_ref):
    for r in range(0, T, ROWS):
        normed, spread = normalize(src_ref[r : r + ROWS, :])
        g = grad_ref[r : r + ROWS, :] * (1.0 + row(mod_ref, scale))
        centered = g - jnp.mean(g, axis=-1, keepdims=True)
        back = spread * (centered - normed * jnp.mean(g * normed, axis=-1, keepdims=True))
        out_ref[r : r + ROWS, :] = (direct_ref[r : r + ROWS, :].astype(f32) + back).astype(bf16)


W_ROWS = 1152
W_CHUNKS = 4 * D // W_ROWS
QKV_CHUNKS = 3 * D // W_ROWS


def weight_copies(w_hbm, w_ref, sems, chunks):
    return [
        pltpu.make_async_copy(
            w_hbm.at[pl.ds(i * W_ROWS, W_ROWS), :],
            w_ref.at[pl.ds((i - chunks[0]) * W_ROWS, W_ROWS), :],
            sems.at[i],
        )
        for i in chunks
    ]


SIDE = HEADS // 2 * HEAD


def qkv_heads(side, w_ref, hid_ref, qk_ref, v_ref):
    for n in range(3):
        start = n * D + side * SIDE
        block = dot(w_ref[start : start + SIDE, :], hid_ref[...], NT)
        for j in range(HEADS // 2):
            h = side * (HEADS // 2) + j
            rows = block[j * HEAD : (j + 1) * HEAD, :]
            if n == 0:
                qk_ref[h, :HEAD] = (rows * (FACTOR * LOG2E)).astype(bf16)
            elif n == 1:
                qk_ref[HEADS + h, :HEAD] = rows.astype(bf16)
            else:
                v_ref[h, :HEAD] = rows.astype(bf16)


def score_grads(q, k, grad_score):
    return dot(k, grad_score) * FACTOR, dot(q, grad_score, NT) * (1.0 / LOG2E)


def grad_heads(w, go, out_ref):
    block = dot(go, w).T
    for h in range(HEADS):
        out_ref[h] = block[h * HEAD : (h + 1) * HEAD, :].astype(bf16)


def spatial_forward_kernel(
    x_ref, cot_hbm, mod_ref, w_hbm,
    both_ref, kept_out, raw_out, inv_ref,
    w_ref, cot_ref, hid_ref, attn_ref, qk_ref, v_ref, o_ref, raw_ref, sems, out_sems,
):
    blocks_of = [(n * D + side * SIDE, SIDE) for side in range(2) for n in range(3)] + [(3 * D, D)]
    copies = [
        pltpu.make_async_copy(w_hbm.at[pl.ds(r, size), :], w_ref.at[pl.ds(r, size), :], sems.at[i])
        for i, (r, size) in enumerate(blocks_of)
    ]
    copies.append(pltpu.make_async_copy(cot_hbm, cot_ref, sems.at[7]))
    for c in copies:
        c.start()
    v_ref[:, HEAD:V_ROWS, :] = jnp.ones((HEADS, V_ROWS - HEAD, T), bf16)
    modulated(x_ref, mod_ref, 0, 1, hid_ref)
    def raw_copy(i):
        part = pl.ds(i * GROUP, GROUP)
        return pltpu.make_async_copy(raw_ref.at[part], raw_out.at[part], out_sems.at[3 + i])

    def group(i, _):
        heads = [i * GROUP + s for s in range(GROUP)]
        scores = [dot(qk_ref[HEADS + h, :HEAD], qk_ref[h, :HEAD], TN) for h in heads]
        raws = []
        for h, sc in zip(heads, scores):
            raws.append(jnp.exp2(sc - jnp.max(sc, axis=0, keepdims=True)).astype(bf16))
            raw_ref[h] = raws[-1]
        raw_copy(i).start()
        for h, raw in zip(heads, raws):
            mixed = dot(v_ref[h], raw)
            inv = 1.0 / mixed[HEAD : HEAD + 1]
            inv_ref[h] = inv
            out = mixed[:HEAD] * inv
            o_ref[h, :HEAD] = out.astype(bf16)
            attn_ref[pl.ds(pl.multiple_of(h * HEAD, 8), HEAD), :] = out
        return _

    for side in range(2):
        for c in copies[3 * side : 3 * side + 3]:
            c.wait()
        qkv_heads(side, w_ref, hid_ref, qk_ref, v_ref)
        lax.fori_loop(side * HEADS // GROUP // 2, (side + 1) * HEADS // GROUP // 2, group, 0)
    kept = [
        pltpu.make_async_copy(qk_ref, kept_out.at[pl.ds(0, 2 * HEADS)], out_sems.at[0]),
        pltpu.make_async_copy(v_ref, kept_out.at[pl.ds(2 * HEADS, HEADS)], out_sems.at[1]),
    ]
    for c in kept:
        c.start()
    kept.append(pltpu.make_async_copy(o_ref, kept_out.at[pl.ds(3 * HEADS, HEADS)], out_sems.at[2]))
    kept[-1].start()
    copies[6].wait()
    copies[7].wait()
    both_ref[:, PLACE:, :] = cot_ref[...].astype(f32).reshape(FRAMES, PLACE, D).astype(bf16)
    block = dot(w_ref[3 * D :, :], attn_ref[...].astype(bf16)).T
    middle = x_ref[...].astype(f32) + row(mod_ref, 2) * block
    both_ref[:, :PLACE, :] = middle.reshape(FRAMES, PLACE, D).astype(bf16)
    for c in kept + [raw_copy(i) for i in range(HEADS // GROUP)]:
        c.wait()


def gather_rows(src_ref, tmp_ref, mine_ref, theirs_ref, rows, start):
    me = lax.axis_index("seq") % 2
    padded = tmp_ref.shape[1]
    tmp_ref[...] = jnp.zeros_like(tmp_ref)
    for core in range(2):
        for chunk in range(SUBS):
            slot = (core * SUBS + chunk) % 2
            for sub in range(SUBS):
                first = rows * owner_of(core, chunk, sub)
                tmp_ref[slot, rows * sub : rows * (sub + 1), :] = src_ref[first : first + rows, :]
            low = tmp_ref[slot].astype(bf16)

            @pl.when(me == core)
            def _(chunk=chunk, low=low):
                mine_ref[chunk, start : start + padded] = low

            @pl.when(me != core)
            def _(chunk=chunk, low=low):
                theirs_ref[chunk, start : start + padded] = low


def by_position(both, start):
    row = lax.broadcasted_iota(jnp.int32, (T, 2 * T), 0)
    col = lax.broadcasted_iota(jnp.int32, (T, 2 * T), 1)
    source = (row % FRAMES) * (2 * PLACE) + row // FRAMES + start
    return dot(jnp.where(source == col, 1.0, 0.0).astype(bf16), both).astype(bf16)


def by_frame(tokens):
    row = lax.broadcasted_iota(jnp.int32, (T, T), 0)
    col = lax.broadcasted_iota(jnp.int32, (T, T), 1)
    source = (row % PLACE) * FRAMES + row // PLACE
    return dot(jnp.where(source == col, 1.0, 0.0).astype(bf16), tokens)


def temporal_kernel(
    both_hbm, mod_ref, w_hbm,
    gm_out, right_ref, mine_ref, theirs_ref,
    w_ref, both_ref, m_ref, cot_ref, gm_ref, hid_ref, qk_ref, v_ref, g_ref, attn_ref, grad_ref, gh_ref,
    tmp_ref, tmp_p_ref, sems,
):
    first = pltpu.make_async_copy(both_hbm, both_ref, sems.at[0])
    weights = pltpu.make_async_copy(w_hbm, w_ref, sems.at[1])
    first.start()
    weights.start()
    first.wait()
    both = both_ref[...].reshape(2 * T, D)
    m_ref[...] = by_position(both, 0)
    modulated(m_ref, mod_ref, 3, 4, hid_ref)
    right_ref[:T, :] = hid_ref[...]
    cot_ref[...] = by_position(both, PLACE)
    go = (cot_ref[...].astype(f32) * row(mod_ref, 5)).astype(bf16)
    grad_ref[:D, :] = go.astype(f32).T
    gather_rows(grad_ref, tmp_p_ref, mine_ref, theirs_ref, P_ROWS, Q_PAD)
    weights.wait()
    for side in range(2):
        qkv_heads(side, w_ref, hid_ref, qk_ref, v_ref)
    grad_heads(w_ref[3 * D :, :], go, g_ref)

    def group(i, _):
        heads = [i * GROUP + s for s in range(GROUP)]
        scores = [blocks(dot(qk_ref[HEADS + h, :HEAD], qk_ref[h, :HEAD], TN)) for h in heads]
        raws = [jnp.exp2(sc - jnp.max(sc, axis=0, keepdims=True)) for sc in scores]
        probs = [raw * (1.0 / jnp.sum(raw, axis=0, keepdims=True)) for raw in raws]
        lows = [spread(prob) for prob in probs]
        grad_probs = [blocks(dot(v_ref[h], g_ref[h], TN)) for h in heads]
        for h, prob, low, gp in zip(heads, probs, lows, grad_probs):
            inner = jnp.sum(prob * gp, axis=0, keepdims=True)
            grad_score = spread(prob * (gp - inner))
            dq, dk = score_grads(qk_ref[h, :HEAD], qk_ref[HEADS + h, :HEAD], grad_score)
            dv = dot(g_ref[h], low, NT)
            attn_ref[pl.ds(pl.multiple_of(h * HEAD, 8), HEAD), :] = dot(v_ref[h], low)
            for n, value in enumerate((dq, dk, dv)):
                grad_ref[pl.ds(pl.multiple_of(n * D + h * HEAD, 8), HEAD), :] = value
        return _

    lax.fori_loop(0, HEADS // GROUP, group, 0)
    gh_ref[...] = dot(grad_ref[...].astype(bf16).T, w_ref[: 3 * D, :])
    norm_back_rows(m_ref, cot_ref, gh_ref, mod_ref, 4, gm_ref)
    gm_out[...] = by_frame(gm_ref[...]).reshape(FRAMES, PLACE, D).astype(bf16)
    right_ref[T:, :] = attn_ref[...].astype(bf16).T
    gather_rows(grad_ref, tmp_ref, mine_ref, theirs_ref, Q_ROWS, 0)


def first_lanes():
    return lax.broadcasted_iota(jnp.int32, (FRAMES, 2 * FRAMES), 1) < FRAMES


def blocks(full):
    f, lane = FRAMES, first_lanes()
    left = jnp.where(lane, full[:f, : 2 * f], full[f : 2 * f, : 2 * f])
    right = jnp.where(lane, full[2 * f : 3 * f, 2 * f :], full[3 * f :, 2 * f :])
    return jnp.concatenate([left, right], axis=1)


def spread(side):
    lane = first_lanes()
    zero = jnp.zeros((FRAMES, 2 * FRAMES), f32)
    a, b = side[:, : 2 * FRAMES], side[:, 2 * FRAMES :]
    left = jnp.concatenate([jnp.where(lane, a, zero), jnp.where(lane, zero, a), zero, zero], axis=0)
    right = jnp.concatenate([zero, zero, jnp.where(lane, b, zero), jnp.where(lane, zero, b)], axis=0)
    return jnp.concatenate([left, right], axis=1).astype(bf16)


def own_bits():
    seq, rep = lax.axis_index("seq"), lax.axis_index("rep")
    core = seq % 2
    ring = (rep * 2 + seq // 32, (seq // 2) % 4, (seq // 8) % 4)
    codes = [v ^ (v >> 1) for v in ring]
    first = [jnp.where(core == 0, v & 1, v >> 1) for v in codes]
    last = [jnp.where(core == 0, v >> 1, v & 1) for v in codes]
    return first, last


def weight_grad_kernel(
    flip, left1_ref, left2_ref, right1_ref, right2_ref, *refs
):
    if flip:
        out0_ref, out1_ref, out2_ref, token_ref, ql_ref, pl_ref, h_ref, a_ref = refs
        token_ref[...] = jnp.zeros_like(token_ref)
        moved = []
    else:
        gm_in, _, out_hbm, gm_out, ql_ref, pl_ref, h_ref, a_ref, out0_ref, out1_ref, out2_ref, sem, out_sems = refs
        passed = pltpu.make_async_copy(gm_in, gm_out, sem)
        passed.start()
        moved = [passed]
    first, _ = own_bits()
    h_ref[:T, :] = right1_ref[:T, :]
    h_ref[T:, :] = right2_ref[:T, :]
    a_ref[:T, :] = right1_ref[T:, :]
    a_ref[T:, :] = right2_ref[T:, :]
    for p, out_ref in enumerate((out0_ref, out1_ref, out2_ref)):
        for i in range(4):
            bits = [None] * 3
            bits[p] = first[p] ^ flip
            bits[(p + 1) % 3] = i >> 1
            bits[(p + 2) % 3] = i & 1
            j = 4 * bits[0] + 2 * bits[1] + bits[2]
            rows = slice(i * Q_PAD, (i + 1) * Q_PAD)
            ql_ref[rows, :T] = left1_ref[j, :Q_PAD]
            ql_ref[rows, T:] = left2_ref[j, :Q_PAD]
            rows = slice(i * P_PAD, (i + 1) * P_PAD)
            pl_ref[rows, :T] = left1_ref[j, Q_PAD:]
            pl_ref[rows, T:] = left2_ref[j, Q_PAD:]
        cols = slice(p * PART, (p + 1) * PART)
        q = dot(ql_ref[...], h_ref[:, cols])
        o = dot(pl_ref[...], a_ref[:, cols])
        for i in range(4):
            out_ref[i] = jnp.concatenate(
                [q[i * Q_PAD : i * Q_PAD + Q_CHUNK], o[i * P_PAD : i * P_PAD + P_CHUNK]], axis=0
            ).astype(bf16)
        if not flip:
            moved.append(pltpu.make_async_copy(out_ref, out_hbm.at[pl.ds(4 * p, 4)], out_sems.at[p]))
            moved[-1].start()
    for c in moved:
        c.wait()


HALF = HEADS // 2


def spatial_attention_back_kernel(
    gm_ref, mod_ref, inv_ref, kept_hbm, raw_hbm, w_hbm, grad_out, token_ref,
    w_ref, g_ref, kept_ref, raw_ref, grad_ref, sems, in_sems,
):
    (weights,) = weight_copies(w_hbm, w_ref, sems, range(QKV_CHUNKS, W_CHUNKS))
    kept = []
    for side in range(2):
        copies = []
        for n in range(4):
            part = pl.ds(n * HEADS + side * HALF, HALF)
            copies.append(pltpu.make_async_copy(kept_hbm.at[part], kept_ref.at[part], in_sems.at[side, n]))
        part = pl.ds(side * HALF, HALF)
        copies.append(pltpu.make_async_copy(raw_hbm.at[part], raw_ref.at[part], in_sems.at[side, 4]))
        kept.append(copies)
    for c in [weights] + kept[0]:
        c.start()
    token_ref[...] = jnp.zeros_like(token_ref)
    go = (gm_ref[...].astype(f32).reshape(T, D) * row(mod_ref, 2)).astype(bf16)
    weights.wait()
    for c in kept[1]:
        c.start()
    grad_heads(w_ref[...], go, g_ref)

    def group(i, _):
        heads = [i * GROUP + s for s in range(GROUP)]
        scaled, grad_probs, inners = [], [], []
        for h in heads:
            g = (g_ref[h].astype(f32) * inv_ref[h]).astype(bf16)
            scaled.append(g)
            out = kept_ref[3 * HEADS + h, :HEAD].astype(f32)
            inners.append(jnp.sum(g.astype(f32) * out, axis=0, keepdims=True))
            grad_probs.append(dot(kept_ref[2 * HEADS + h, :HEAD], g, TN))
        for h, g, inner, gp in zip(heads, scaled, inners, grad_probs):
            raw = raw_ref[h]
            grad_score = (raw.astype(f32) * (gp - inner)).astype(bf16)
            dq, dk = score_grads(kept_ref[h, :HEAD], kept_ref[HEADS + h, :HEAD], grad_score)
            for n, value in enumerate((dq, dk, dot(g, raw, NT))):
                grad_ref[pl.ds(pl.multiple_of(n * D + h * HEAD, 8), HEAD), :] = value
        return _

    for side in range(2):
        for c in kept[side]:
            c.wait()
        lax.fori_loop(side * HALF // GROUP, (side + 1) * HALF // GROUP, group, 0)
    grad_out[...] = grad_ref[...].astype(bf16)


def spatial_norm_back_kernel(
    grad_ref, gm_hbm, x_hbm, mod_ref, w_hbm, out_ref, token_ref, w_ref, gh_ref, gm_in, gm_ref, x_ref, sems, in_sems
):
    copies = weight_copies(w_hbm, w_ref, sems, range(QKV_CHUNKS))
    copies.append(pltpu.make_async_copy(gm_hbm, gm_in, in_sems.at[0]))
    copies.append(pltpu.make_async_copy(x_hbm, x_ref, in_sems.at[1]))
    for c in copies:
        c.start()
    token_ref[...] = jnp.zeros_like(token_ref)
    flipped = grad_ref[...].T
    copies[0].wait()
    copies[1].wait()
    gh_ref[...] = dot(flipped[:, : 2 * D], w_ref[: 2 * D, :])
    for c in copies[2:]:
        c.wait()
    gm_ref[...] = gm_in[...].astype(f32).reshape(T, D).astype(bf16)
    gh_ref[...] = gh_ref[...] + dot(flipped[:, 2 * D :], w_ref[2 * D :, :])
    norm_back_rows(x_ref, gm_ref, gh_ref, mod_ref, 1, out_ref)


def chunk_bits():
    first, _ = own_bits()
    return [(first[(p + 1) % 3], first[(p + 2) % 3]) for p in range(3)]


def second_sums_kernel(flip, *refs):
    keep_hbm, got, out, keep, sems = refs[0], refs[1:4], refs[4:7], refs[7:10], refs[10]
    bits = [a ^ flip for a, _ in chunk_bits()]
    copies = [
        pltpu.make_async_copy(keep_hbm.at[pl.ds(4 * p + 2 * a, 2)], keep[p], sems.at[p])
        for p, a in enumerate(bits)
    ]
    for c in copies:
        c.start()
    for p, a in enumerate(bits):
        copies[p].wait()
        for j in range(2):
            out[p][j] = (keep[p][j].astype(f32) + got[p][2 * a + j].astype(f32)).astype(bf16)


def third_send_kernel(*refs):
    keep, got, own, out = refs[0:3], refs[3:6], refs[6:9], refs[9:12]
    for p, (_, b) in enumerate(chunk_bits()):
        for to, i in ((out, 1 - b), (own, b)):
            to[p][...] = (keep[p][i].astype(f32) + got[p][i].astype(f32)).astype(bf16)


def xor_pairs(flips):
    pairs = []
    for coord in all_coords():
        other = list(coord)
        for axis in range(2):
            if (flips >> (1 - axis)) & 1:
                other[axis] = GRAY.index(GRAY[coord[axis]] ^ (1 << (1 - coord[3])))
        pairs.append((device_index(*coord), device_index(*other)))
    return pairs


def split_rows(total_ref, count, part_ref):
    rows = total_ref.shape[0]
    q_rows = rows * Q_ROWS // (Q_ROWS + P_ROWS) // count
    p_rows = rows // count - q_rows
    for k in range(count):
        p = count * q_rows + k * p_rows
        part_ref[k, :q_rows] = total_ref[k * q_rows : (k + 1) * q_rows, :]
        part_ref[k, q_rows:] = total_ref[p : p + p_rows, :]


def fourth_send_kernel(*refs):
    keep, got = refs[0:3], refs[3:6]
    own_ref, sends, row_ref, part_ref = refs[7], refs[8:11], refs[11], refs[12]
    for p in range(3):
        row_ref[:, p * PART : (p + 1) * PART] = keep[p][...].astype(f32) + got[p][...].astype(f32)
    split_rows(row_ref, 4, part_ref)
    _, last = own_bits()
    me = 2 * last[0] + last[1]
    own_ref[...] = part_ref[me]
    for d in range(1, 4):
        sends[d - 1][...] = part_ref[me ^ d].astype(bf16)


def fifth_send_kernel(own_in, got1_ref, got2_ref, got3_ref, _, own_ref, send_ref, row_ref, part_ref):
    row_ref[...] = (own_in[...] + got1_ref[...].astype(f32)) + (
        got2_ref[...].astype(f32) + got3_ref[...].astype(f32)
    )
    split_rows(row_ref, 2, part_ref)
    _, last = own_bits()
    own_ref[...] = part_ref[last[2]]
    send_ref[...] = part_ref[1 - last[2]].astype(bf16)


def last_sum_kernel(own_ref, got_ref, q_ref, p_ref):
    total = own_ref[...] + got_ref[...].astype(f32)
    q_ref[...] = total[:Q_ROWS]
    p_ref[...] = total[Q_ROWS:]


VMEM = pl.BlockSpec(memory_space=pltpu.VMEM)
ANY = pl.BlockSpec(memory_space=pl.ANY)


def call(kernel, outs, scratch, specs, flops, name, out_specs=None, limit=54):
    return pl.pallas_call(
        kernel,
        out_shape=[jax.ShapeDtypeStruct(s, d) for s, d in outs],
        in_specs=specs,
        out_specs=out_specs or [VMEM] * len(outs),
        scratch_shapes=scratch,
        compiler_params=pltpu.CompilerParams(vmem_limit_bytes=limit * 1024 * 1024),
        cost_estimate=pl.CostEstimate(flops=flops, bytes_accessed=12_000_000 if flops > 1_000_000_000 else 1_000, transcendentals=0),
        name=name,
    )


WEIGHT = pltpu.VMEM((4 * D, D), bf16)
TOKEN = ((8, 128), f32)
W_OUT = pltpu.VMEM((D, D), bf16)
SEMS = pltpu.SemaphoreType.DMA((W_CHUNKS,))
QK = ((2 * HEADS, V_ROWS, T), bf16)
V = ((HEADS, V_ROWS, T), bf16)
HEAD_ROWS = ((HEADS, HEAD, T), bf16)
TOKENS = ((T, D), bf16)


RAW = ((HEADS, T, T), bf16)


def spatial_forward(x, cot, mod, w):
    return call(
        spatial_forward_kernel,
        [((FRAMES, 2 * PLACE, D), bf16), KEPT, KEPT_RAW, ((HEADS, 1, T), f32)],
        [
            WEIGHT,
            pltpu.VMEM(*TOKENS),
            pltpu.VMEM(*TOKENS),
            pltpu.VMEM((D, T), f32),
            pltpu.VMEM(*QK),
            pltpu.VMEM(*V),
            pltpu.VMEM(*V),
            pltpu.VMEM(*RAW),
            pltpu.SemaphoreType.DMA((8,)),
            pltpu.SemaphoreType.DMA((3 + HEADS // GROUP,)),
        ],
        [VMEM, ANY, VMEM, ANY],
        6_000_000_000,
        "spatial_forward",
        [VMEM, ANY, ANY, VMEM],
    )(x, cot, mod, w)


LEFT = ((SUBS, Q_PAD + P_PAD, T), bf16)
RIGHT = ((2 * T, D), bf16)


def temporal(both, mod, w):
    return call(
        temporal_kernel,
        [((FRAMES, PLACE, D), bf16), RIGHT, LEFT, LEFT],
        [
            WEIGHT,
            pltpu.VMEM((FRAMES, 2 * PLACE, D), bf16),
            pltpu.VMEM(*TOKENS),
            pltpu.VMEM(*TOKENS),
            pltpu.VMEM(*TOKENS),
            pltpu.VMEM(*TOKENS),
            pltpu.VMEM(*QK),
            pltpu.VMEM(*HEAD_ROWS),
            pltpu.VMEM(*HEAD_ROWS),
            pltpu.VMEM((D, T), f32),
            pltpu.VMEM((3 * D, T), f32),
            pltpu.VMEM((T, D), f32),
            pltpu.VMEM((2, Q_PAD, T), f32),
            pltpu.VMEM((2, P_PAD, T), f32),
            pltpu.SemaphoreType.DMA((2,)),
        ],
        [ANY, VMEM, ANY],
        12_000_000_000,
        "temporal_sublayer",
        limit=40,
    )(both, mod, w)


def weight_grad(flip, *operands):
    part = ((4, CHUNK, PART), bf16)
    scratch = [
        pltpu.VMEM((4 * Q_PAD, 2 * T), bf16),
        pltpu.VMEM((4 * P_PAD, 2 * T), bf16),
        pltpu.VMEM((2 * T, D), bf16),
        pltpu.VMEM((2 * T, D), bf16),
    ]
    if not flip:
        scratch += [pltpu.VMEM(*part)] * 3 + [pltpu.SemaphoreType.DMA, pltpu.SemaphoreType.DMA((3,))]
    return call(
        functools.partial(weight_grad_kernel, flip),
        [part] * 3 + [TOKEN] if flip else [KEPT_SUMS, ((FRAMES, PLACE, D), bf16)],
        scratch,
        [VMEM] * 4 + [ANY] * (2 - 2 * flip),
        10_000_000,
        "weight_grad_send" if flip else "weight_grad_keep",
        [VMEM] * 4 if flip else [ANY] * 2,
        limit=20,
    )(*operands)


def spatial_attention_back(gm, mod, kept, raw, inv, w):
    return call(
        spatial_attention_back_kernel,
        [((3 * D, T), bf16), TOKEN],
        [
            W_OUT,
            pltpu.VMEM(*HEAD_ROWS),
            pltpu.VMEM((4 * HEADS, V_ROWS, T), bf16),
            pltpu.VMEM(*RAW),
            pltpu.VMEM((3 * D, T), f32),
            SEMS,
            pltpu.SemaphoreType.DMA((2, 5)),
        ],
        [VMEM] * 3 + [ANY] * 3,
        5_000_000_000,
        "spatial_attention_back",
        limit=51,
    )(gm, mod, inv, kept, raw, w)


def spatial_norm_back(grad, gm, x, mod, w):
    return call(
        spatial_norm_back_kernel,
        [TOKENS, TOKEN],
        [
            pltpu.VMEM((3 * D, D), bf16),
            pltpu.VMEM((T, D), f32),
            pltpu.VMEM((FRAMES, PLACE, D), bf16),
            pltpu.VMEM(*TOKENS),
            pltpu.VMEM(*TOKENS),
            SEMS,
            pltpu.SemaphoreType.DMA((2,)),
        ],
        [VMEM, ANY, ANY, VMEM, ANY],
        5_000_000_000,
        "spatial_norm_back",
        limit=51,
    )(grad, gm, x, mod, w)


def reduce_rows(send, keep, tokens):
    half, one = ((2, CHUNK, PART), bf16), ((CHUNK, PART), bf16)

    def second_sums(flip):
        return call(
            functools.partial(second_sums_kernel, flip),
            [half] * 3,
            [pltpu.VMEM(*half)] * 3 + [pltpu.SemaphoreType.DMA((3,))],
            [ANY] + [VMEM] * 3,
            1_000_000,
            "second_sums_send" if flip else "second_sums_own",
            limit=16,
        )(keep, *got)

    got = [lax.ppermute(send[p], BOTH, flip_pairs(p, (0, 1))) for p in range(3)]
    out, own = second_sums(1), second_sums(0)
    got = [lax.ppermute(out[p], BOTH, flip_pairs((p + 1) % 3, (0, 1))) for p in range(3)]
    outs = call(third_send_kernel, [one] * 6, [], [VMEM] * 6, 1_000_000, "third_send", limit=12)(*own, *got)
    own, out = outs[:3], outs[3:]
    got = [lax.ppermute(out[p], BOTH, flip_pairs((p + 2) % 3, (0, 1))) for p in range(3)]
    rows = CHUNK // 4
    own, *out = call(
        fourth_send_kernel,
        [((rows, D), f32)] + [((rows, D), bf16)] * 3,
        [pltpu.VMEM((CHUNK, D), f32), pltpu.VMEM((4, rows, D), f32)],
        [VMEM] * 6 + [ANY],
        1_000_000,
        "fourth_send",
        limit=16,
    )(*own, *got, tokens[0])
    moved = [lax.ppermute(out[d - 1], BOTH, xor_pairs(d)) for d in range(1, 4)]
    own, sent = call(
        fifth_send_kernel,
        [((rows // 2, D), f32), ((rows // 2, D), bf16)],
        [pltpu.VMEM((rows, D), f32), pltpu.VMEM((2, rows // 2, D), f32)],
        [VMEM] * 4 + [ANY],
        1_000_000,
        "fifth_send",
        limit=8,
    )(own, *moved, tokens[1])
    moved = lax.ppermute(sent, BOTH, flip_pairs(2, (1, 0)))
    return call(
        last_sum_kernel,
        [((Q_ROWS, D), f32), ((P_ROWS, D), f32)],
        [],
        [VMEM] * 2,
        1_000_000,
        "last_sum",
        limit=8,
    )(own, moved)


def on_device(clip_tokens, modulation, spatial_weights, temporal_weights, out_cotangent):
    x = clip_tokens.reshape(T, D)
    cot = out_cotangent.reshape(T, D)
    mod = modulation.reshape(6, 1, D)
    both, kept, raw, inv = spatial_forward(x, cot, mod, spatial_weights)
    both_pos = lax.all_to_all(both, "seq", 0, 0, tiled=True)
    gm_pos, right, left, theirs = temporal(both_pos, mod, temporal_weights)
    operands = (left, lax.ppermute(theirs, BOTH, core_pairs()), right, lax.ppermute(right, BOTH, core_pairs()))
    *send, token = weight_grad(1, *operands)
    keep, gm_pos = weight_grad(0, *operands, gm_pos, token)
    gm = lax.all_to_all(gm_pos, "seq", 0, 0, tiled=True)
    grad, token1 = spatial_attention_back(gm, mod, kept, raw, inv, spatial_weights)
    input_grad, token2 = spatial_norm_back(grad, gm, x, mod, spatial_weights)
    tokens = (token1, token2)
    qkv_rows, proj_rows = reduce_rows(send, keep, tokens)
    return input_grad.reshape(clip_tokens.shape), qkv_rows, proj_rows


def solution(mesh):
    placed = (
        P("rep", "seq", None, None),
        P("rep", None, None),
        P(),
        P(),
        P("rep", "seq", None, None),
    )
    return jax.shard_map(
        on_device,
        mesh=mesh,
        in_specs=placed,
        out_specs=(P("rep", "seq", None, None), P(BOTH, None), P(BOTH, None)),
        check_vma=False,
    )
```
